128 devices in a mesh: wide: 8 (over x, core), narrow: 16 (over z, y).
Axes of the slice: x: 4, y: 4, z: 4, core: 2. Of those that a mesh axis runs over, the one named last changes fastest.
Arguments:
- view_a: bfloat16 [1024, 8192], P(('wide', 'narrow')), may hold values from -20000 to 20000, as said below
- view_b: bfloat16 [1024, 8192], P(('wide', 'narrow')), may hold values from -20000 to 20000
Outputs:
- corr: bfloat16 [8192, 8192], P('wide', 'narrow')
- loss_value: float32 [], replicated
- grad_a: bfloat16 [1024, 8192], P(('wide', 'narrow'))
- grad_b: bfloat16 [1024, 8192], P(('wide', 'narrow'))
The draws below stay inside these ranges and needn't reach their ends.
Inputs may be any that keep to these rules, and one draw needn't show every extreme that they name: view_b shows the same images as view_a under another augmentation.
All inputs are finite; a program needn't handle non-finite values.
Results may differ from the reference program's by a relative error of at most 0.019.
Values may be sent and summed in bfloat16 or wider, within the bound.
A program may use at most 64 MiB of HBM per device.

```python
import jax
import jax.numpy as jnp
from jax import lax

FEAT = 8192
ROWS_DEV = 8
BATCH = 1024


def paired_views(key):
    keys = jax.random.split(jax.random.fold_in(key, 11), 12)
    row_pos = jnp.arange(BATCH, dtype=jnp.float32)
    member = (jnp.arange(BATCH) // ROWS_DEV % 4).astype(jnp.float32)
    lift = 0.35
    offset_range = 0.6
    content = jax.random.truncated_normal(keys[0], -4.0, 4.0, (BATCH, FEAT), jnp.float32)
    other = jax.random.truncated_normal(keys[1], -4.0, 4.0, (BATCH, FEAT), jnp.float32)
    exponent = lift * row_pos / BATCH + lift * member / 3.0 + 0.3 * jax.random.uniform(keys[2], (BATCH,), jnp.float32)
    row_scale = 10.0 ** exponent
    envelope = 0.15 + 0.85 * jnp.arange(FEAT, dtype=jnp.float32) / FEAT
    loads = jax.random.truncated_normal(keys[3], -4.0, 4.0, (4, FEAT), jnp.float32) * envelope
    loads = loads * jax.random.uniform(keys[4], (FEAT,), jnp.float32, 0.6, 1.4)
    shared = jax.random.truncated_normal(keys[5], -4.0, 4.0, (BATCH, 4), jnp.float32)
    factor_a = shared + 0.3 * jax.random.truncated_normal(keys[6], -4.0, 4.0, (BATCH, 4), jnp.float32)
    factor_b = shared + 0.3 * jax.random.truncated_normal(keys[7], -4.0, 4.0, (BATCH, 4), jnp.float32)
    mixed_a = content
    mixed_b = 0.7 * content + 0.71 * other
    for number in range(4):
        mixed_a = mixed_a + factor_a[:, number:number + 1] * loads[number]
        mixed_b = mixed_b + factor_b[:, number:number + 1] * loads[number]
    scale_a = 10.0 ** jax.random.uniform(keys[8], (FEAT,), jnp.float32)
    scale_b = 10.0 ** jax.random.uniform(keys[9], (FEAT,), jnp.float32)
    offset_a = jax.random.uniform(keys[10], (FEAT,), jnp.float32, -offset_range, offset_range)
    offset_b = jax.random.uniform(keys[11], (FEAT,), jnp.float32, -offset_range, offset_range)
    first_view = row_scale[:, None] * scale_a * (mixed_a + offset_a)
    second_view = row_scale[:, None] * scale_b * (mixed_b + offset_b)
    return (first_view, second_view)


def draw_view_a(key, part):
    return paired_views(key)[0].astype(jnp.bfloat16)


def draw_view_b(key, part):
    return paired_views(key)[1].astype(jnp.bfloat16)


def setup_inputs(seed: int = 0) -> dict:
    streams_of = jax.random.split(jax.random.key(seed), 3)
    return {
        "view_a": draw_view_a(jax.random.fold_in(streams_of[2], 71), 0),
        "view_b": draw_view_b(jax.random.fold_in(streams_of[2], 71), 0),
    }


off_weight = 0.0051
epsilon = 1e-05

def standardize(view):
    samples = view.shape[0]
    floats = view.astype(jnp.float32)
    average = lax.optimization_barrier(jnp.sum(floats, axis=0)) / samples
    variance = lax.optimization_barrier(jnp.sum(floats * floats, axis=0)) / samples - average * average
    inv_std = lax.rsqrt(variance + epsilon)
    return (((floats - average) * inv_std).astype(jnp.bfloat16), inv_std)

def normalize_back(dstd, std_view, inv_std):
    samples = dstd.shape[0]
    floats = std_view.astype(jnp.float32)
    first_moment = lax.optimization_barrier(jnp.sum(dstd, axis=0)) / samples
    second_moment = lax.optimization_barrier(jnp.sum(dstd * floats, axis=0)) / samples
    return (inv_std * (dstd - first_moment - floats * second_moment)).astype(jnp.bfloat16)

def reference(view_a, view_b):
    samples = view_a.shape[0]
    std_a, inv_a = standardize(view_a)
    std_b, inv_b = standardize(view_b)
    cross_corr = lax.dot_general(std_a, std_b, (((0,), (0,)), ((), ())), preferred_element_type=jnp.float32) / samples
    position = jnp.arange(FEAT)
    diagonal = position[:, None] == position[None, :]
    loss_value = jnp.sum(jnp.where(diagonal, (1.0 - cross_corr) * (1.0 - cross_corr), off_weight * cross_corr * cross_corr)) / FEAT
    diag_mask = diagonal.astype(jnp.float32)
    weights = (2.0 * off_weight * cross_corr + diag_mask * (-2.0 * (1.0 - cross_corr) - 2.0 * off_weight * cross_corr)).astype(jnp.bfloat16)
    dstd_a = lax.dot_general(std_b, weights, (((1,), (1,)), ((), ())), preferred_element_type=jnp.float32)
    dstd_b = jnp.dot(std_a, weights, preferred_element_type=jnp.float32)
    grad_a = normalize_back(dstd_a, std_a, inv_a)
    grad_b = normalize_back(dstd_b, std_b, inv_b)
    return (cross_corr.astype(jnp.bfloat16), loss_value, grad_a, grad_b)
```

```python
import functools

import jax
import jax.numpy as jnp
from jax import lax
from jax.experimental import pallas as pl
from jax.experimental.pallas import tpu as pltpu
from jax.sharding import PartitionSpec as P

off_weight = 0.0051
epsilon = 1e-05
MESH = pl.DeviceIdType.MESH
F32 = jnp.float32
BF16 = jnp.bfloat16


def kernel(
    WN, NN, BLK, SAMPLES,
    a_ref, b_ref,
    corr_ref, loss_ref, ga_ref, gb_ref,
    xa, xb, xb2, xa2,
    A3, B3, b1w, a1n,
    S_a, S_b, SR_a,
    gas, gar, gaall, gbs, gbr, gball,
    va, vb, Dn, Dw,
    dA, dB,
    mas, mar, mbs, mbr,
    ras, rar, rbs, rbr,
    lbuf, lsend, lrecv, corr_v,
    s_w, r_w, s_n, r_n, corr_sem,
):
    SLAB = BLK * (NN // WN)
    HB, HS = BLK // 2, SLAB // 2
    HN = SAMPLES // 2
    FEATS = BLK * NN
    w = lax.axis_index("wide")
    n = lax.axis_index("narrow")
    diag = lax.div(n, 2) == w

    def wide_copy(which, k, src, dst):
        return pltpu.make_async_remote_copy(
            src_ref=src, dst_ref=dst,
            send_sem=s_w.at[which, k], recv_sem=r_w.at[which, k],
            device_id=(lax.rem(w + k, WN), n), device_id_type=MESH,
        )

    def narrow_copy(which, k, src, dst):
        return pltpu.make_async_remote_copy(
            src_ref=src, dst_ref=dst,
            send_sem=s_n.at[which, k], recv_sem=r_n.at[which, k],
            device_id=(w, lax.rem(n + k, NN)), device_id_type=MESH,
        )

    def each(count, body):
        def step(k, c):
            body(k)
            return c
        lax.fori_loop(1, count, step, 0)

    def wide_a2a(which, src, dst):
        each(WN, lambda k: wide_copy(which, k, src.at[lax.rem(w + k, WN)], dst.at[w]).start())

    def narrow_a2a(which, src, dst):
        each(NN, lambda k: narrow_copy(which, k, src.at[lax.rem(n + k, NN)], dst.at[n]).start())

    def wide_bcast(which, src, dst):
        each(WN, lambda k: wide_copy(which, k, src, dst.at[w]).start())

    def narrow_bcast(which, src, dst):
        each(NN, lambda k: narrow_copy(which, k, src, dst.at[n]).start())

    def wide_recv(which, dst):
        each(WN, lambda k: wide_copy(which, k, dst.at[0], dst.at[0]).wait_recv())

    def narrow_recv(which, dst):
        each(NN, lambda k: narrow_copy(which, k, dst.at[0], dst.at[0]).wait_recv())

    def wide_sent(which, src):
        each(WN, lambda k: wide_copy(which, k, src, src).wait_send())

    def narrow_sent(which, src):
        each(NN, lambda k: narrow_copy(which, k, src, src).wait_send())

    barrier = pltpu.get_barrier_semaphore()
    each(WN, lambda k: pl.semaphore_signal(
        barrier, inc=1, device_id=(lax.rem(w + k, WN), n), device_id_type=MESH))
    each(NN, lambda k: pl.semaphore_signal(
        barrier, inc=1, device_id=(w, lax.rem(n + k, NN)), device_id_type=MESH))

    def stack(ref, base, half):
        return jnp.concatenate(
            [ref[:, base:base + half], ref[:, base + half:base + 2 * half]], axis=0)

    for i in range(WN):
        xa[i] = stack(a_ref, i * SLAB, HS)
    for i in range(NN):
        xb[i] = stack(b_ref, i * BLK, HB)
    pl.semaphore_wait(barrier, WN + NN - 2)

    wide_a2a(0, xa, A3.at[n])
    narrow_a2a(0, xb, B3.at[w])
    A3[n, w] = xa[w]
    B3[w, n] = xb[n]
    for i in range(WN):
        xb2[i] = stack(b_ref, i * SLAB, HS)
    for i in range(NN):
        xa2[i] = stack(a_ref, i * BLK, HB)
    b1w[w] = xb2[w]
    a1n[n] = xa2[n]
    wide_recv(0, A3.at[n])
    narrow_bcast(1, A3.at[n], A3)
    narrow_recv(0, B3.at[w])
    wide_bcast(1, B3.at[w], B3)
    wide_a2a(2, xb2, b1w)
    narrow_a2a(2, xa2, a1n)

    def add_sums(ref, sums):
        def step(i, c):
            v = ref[i].astype(F32)
            return (c[0] + v, c[1] + v * v)
        return lax.fori_loop(0, ref.shape[0], step, sums, unroll=4)

    def moments_of(sums):
        total, squares = sums

        def fold(t):
            return [jnp.sum(t[h * 8:(h + 1) * 8], axis=0, keepdims=True) / SAMPLES for h in (0, 1)]
        means, seconds = fold(total), fold(squares)
        invs = [lax.rsqrt(q - m * m + epsilon) for q, m in zip(seconds, means)]
        return means, invs

    def stacked(halves):
        return jnp.concatenate([jnp.broadcast_to(h, (8, h.shape[1])) for h in halves], axis=0)

    zero = jnp.zeros((16, HB), F32)
    sums = add_sums(B3.at[w], (zero, zero))

    def arrive_b(k, c):
        wide_copy(1, k, B3.at[0], B3.at[0]).wait_recv()
        return add_sums(B3.at[lax.rem(w - k + WN, WN)], c)
    sums = lax.fori_loop(1, WN, arrive_b, sums)
    mean_b, inv_b = moments_of(sums)
    mean2, inv2 = stacked(mean_b), stacked(inv_b)

    def norm_b(i, c):
        src, pair = lax.div(i, NN // 2), lax.rem(i, NN // 2)
        even = (B3[src, 2 * pair].astype(F32) - mean2) * inv2
        odd = (B3[src, 2 * pair + 1].astype(F32) - mean2) * inv2
        at = pl.ds(pl.multiple_of(i * 16, 16), 16)
        for h in (0, 1):
            S_b[at, h * HB:(h + 1) * HB] = jnp.concatenate(
                [even[h * 8:h * 8 + 8], odd[h * 8:h * 8 + 8]], axis=0).astype(BF16)
        return c
    lax.fori_loop(0, SAMPLES // 16, norm_b, 0, unroll=2)

    dot_last = functools.partial(
        lax.dot_general, dimension_numbers=(((1,), (1,)), ((), ())), preferred_element_type=F32)

    def stack_gram(dst, g):
        count = g.shape[0] // 8
        g3 = g.reshape(count, 8, SAMPLES)
        dst[...] = jnp.concatenate([g3[:, :, :HN], g3[:, :, HN:]], axis=1).astype(BF16)

    own_rows = S_b[pl.ds(pl.multiple_of(w * NN * 8, 16), NN * 8), :]
    stack_gram(gbs, dot_last(own_rows, S_b[...]))
    narrow_a2a(3, gbs, gbr)
    gbr[n] = gbs[n]

    zero = jnp.zeros((16, HS), F32)
    sums = add_sums(A3.at[n], (zero, zero))

    def arrive_a(k, c):
        narrow_copy(1, k, A3.at[0], A3.at[0]).wait_recv()
        return add_sums(A3.at[lax.rem(n - k + NN, NN)], c)
    sums = lax.fori_loop(1, NN, arrive_a, sums)
    mean_a, inv_a = moments_of(sums)
    mean2a, inv2a = stacked(mean_a), stacked(inv_a)

    def norm_a(i, c):
        src, pair = lax.div(i, NN // 2), lax.rem(i, NN // 2)
        even = (A3[2 * pair, src].astype(F32) - mean2a) * inv2a
        odd = (A3[2 * pair + 1, src].astype(F32) - mean2a) * inv2a
        at = pl.ds(pl.multiple_of(i * 16, 16), 16)
        for h in (0, 1):
            S_a[at, h * HS:(h + 1) * HS] = jnp.concatenate(
                [even[h * 8:h * 8 + 8], odd[h * 8:h * 8 + 8]], axis=0).astype(BF16)
        return c
    lax.fori_loop(0, SAMPLES // 16, norm_a, 0)
    for i in range(WN // 2):
        even = (A3[n, 2 * i].astype(F32) - mean2a) * inv2a
        odd = (A3[n, 2 * i + 1].astype(F32) - mean2a) * inv2a
        for h in (0, 1):
            SR_a[i * 16:i * 16 + 16, h * HS:(h + 1) * HS] = jnp.concatenate(
                [even[h * 8:h * 8 + 8], odd[h * 8:h * 8 + 8]], axis=0).astype(BF16)

    stack_gram(gas, dot_last(SR_a[...], S_a[...]))
    wide_a2a(3, gas, gar)
    gar[w] = gas[w]

    half = lax.rem(n, 2)
    lbuf[...] = jnp.zeros_like(lbuf)

    @pl.when(diag)
    def _():
        def step(i, c):
            at = pl.ds(pl.multiple_of(i * 16, 16), 16)
            cols = pl.ds(pl.multiple_of(half * BLK, BLK), BLK)
            return c + S_a[at, cols].astype(F32) * S_b[at, :].astype(F32)
        prod = lax.fori_loop(0, SAMPLES // 16, step, jnp.zeros((16, BLK), F32), unroll=4)
        c = jnp.sum(prod, axis=0, keepdims=True) / SAMPLES
        d = -2.0 * (1.0 - c) - 2.0 * off_weight * c
        mb = jnp.concatenate(mean_b, axis=1)
        ib = jnp.concatenate(inv_b, axis=1)
        first = (half == 0).astype(F32)
        ma = mean_a[0] * first + mean_a[1] * (1.0 - first)
        ia = inv_a[0] * first + inv_a[1] * (1.0 - first)
        pad = jnp.zeros((5, BLK), F32)
        va[...] = jnp.concatenate([ma, ia, d, pad], axis=0)
        vb[...] = jnp.concatenate([mb, ib, d, pad], axis=0)
        Dn[...] = va[...]
        Dw[half] = vb[...]
        lbuf[0:1, :] = (1.0 - c) * (1.0 - c) - off_weight * c * c
        each(WN, lambda k: wide_copy(4, k, va, Dn).start())
        each(NN, lambda k: narrow_copy(4, k, vb, Dw.at[half]).start())

    narrow_recv(3, gbr)

    def total_of(ref):
        t = ref[0].astype(F32)
        for i in range(1, ref.shape[0]):
            t = t + ref[i].astype(F32)
        return t
    gball[w] = total_of(gbr).astype(BF16)
    wide_bcast(5, gball.at[w], gball)

    TM = 256 if SLAB % 256 == 0 else SLAB

    def corr_out(i):
        at = pl.ds(pl.multiple_of(i * TM, TM), TM)
        return pltpu.make_async_copy(corr_v.at[at, :], corr_ref.at[at, :], corr_sem.at[i])

    def cross_tile(i, acc):
        at = pl.ds(pl.multiple_of(i * TM, TM), TM)
        c = lax.dot_general(
            S_a[:, at], S_b[...], (((0,), (0,)), ((), ())), preferred_element_type=F32
        ) * (1.0 / SAMPLES)
        corr_v[at, :] = c.astype(BF16)
        corr_out(i).start()
        return acc + jnp.sum((c * c).reshape(TM // 8, 8, BLK), axis=0)
    tiles = SLAB // TM
    acc = lax.fori_loop(0, 1, cross_tile, jnp.zeros((8, BLK), F32))

    wide_recv(3, gar)
    gaall[n] = total_of(gar).astype(BF16)
    narrow_bcast(5, gaall.at[n], gaall)
    acc = lax.fori_loop(1, tiles, cross_tile, acc)
    lbuf[...] = lbuf[...] + off_weight * acc

    wide_recv(2, b1w)
    narrow_recv(2, a1n)

    @pl.when(lax.div(n, 2) != w)
    def _():
        wide_copy(4, lax.rem(w - lax.div(n, 2) + WN, WN), va, Dn).wait_recv()
    for h in (0, 1):
        @pl.when(n != 2 * w + h)
        def _():
            narrow_copy(4, lax.rem(n - 2 * w - h + NN, NN), vb, Dw.at[h]).wait_recv()

    vec = lambda r, i: [Dw[h, i:i + 1, :] for h in (0, 1)]
    dmean, dinv, dd = (stacked([Dw[h, i:i + 1, :] for h in (0, 1)]) for i in range(3))
    for i in range(WN):
        s = ((b1w[i].astype(F32) - dmean) * dinv).astype(BF16).astype(F32) * dd
        for h in (0, 1):
            dA[i * 8:i * 8 + 8, h * HS:(h + 1) * HS] = s[h * 8:h * 8 + 8]
    dmean, dinv, dd = (
        stacked([Dn[i:i + 1, h * HB:(h + 1) * HB] for h in (0, 1)]) for i in range(3))
    for i in range(NN):
        s = ((a1n[i].astype(F32) - dmean) * dinv).astype(BF16).astype(F32) * dd
        for h in (0, 1):
            dB[i * 8:i * 8 + 8, h * HB:(h + 1) * HB] = s[h * 8:h * 8 + 8]

    factor = 2.0 * off_weight / SAMPLES

    def unstack(ref):
        g = ref[...].astype(F32)
        rows = ref.shape[0] * 8
        return [g[:, h * 8:h * 8 + 8, :].reshape(rows, HN).astype(BF16) for h in (0, 1)]

    def sum_messages(ref):
        t = ref[0]
        for i in range(1, ref.shape[0]):
            t = t + ref[i]
        return t

    wide_recv(5, gball)
    g0, g1 = unstack(gball)
    Q = SLAB // 4
    d = factor * (
        jnp.dot(g0, S_a[:HN, :], preferred_element_type=F32)
        + jnp.dot(g1, S_a[HN:, :], preferred_element_type=F32)
    ) + dA[...]
    dA[...] = d
    m1 = jnp.sum(d, axis=0, keepdims=True)
    m2 = jnp.sum(d * SR_a[...].astype(F32), axis=0, keepdims=True)
    mas[0:8, :] = jnp.concatenate(
        [m[:, q * Q:(q + 1) * Q] for m in (m1, m2) for q in range(4)], axis=0)
    mas[8:16, :] = lbuf[:, :BLK // 2] + lbuf[:, BLK // 2:]
    narrow_bcast(6, mas, mar)
    mar[n] = mas[...]

    narrow_recv(5, gaall)
    g0, g1 = unstack(gaall)
    own = pl.ds(pl.multiple_of(w * NN * 8, 16), NN * 8)
    d = factor * (
        jnp.dot(g0, S_b[:HN, :], preferred_element_type=F32)
        + jnp.dot(g1, S_b[HN:, :], preferred_element_type=F32)
    ) + dB[...]
    dB[...] = d
    m1 = jnp.sum(d, axis=0, keepdims=True)
    m2 = jnp.sum(d * S_b[own, :].astype(F32), axis=0, keepdims=True)
    QB = BLK // 4
    mbs[...] = jnp.concatenate(
        [m[:, q * QB:(q + 1) * QB] for m in (m1, m2) for q in range(4)], axis=0)
    wide_bcast(6, mbs, mbr)
    mbr[w] = mbs[...]

    narrow_recv(6, mar)
    total = sum_messages(mar) / SAMPLES
    m1 = jnp.concatenate([total[q:q + 1] for q in range(4)], axis=1)
    m2 = jnp.concatenate([total[q + 4:q + 5] for q in range(4)], axis=1)
    inv = jnp.concatenate(inv_a, axis=1)
    grad = inv * (dA[...] - m1 - SR_a[...].astype(F32) * m2)
    for i in range(WN):
        ras[i] = jnp.concatenate(
            [grad[i * 8:i * 8 + 8, h * HS:(h + 1) * HS] for h in (0, 1)], axis=0).astype(BF16)
    wide_a2a(7, ras, rar)
    rar[w] = ras[w]
    lsend[...] = total[8:16] * SAMPLES
    wide_bcast(8, lsend, lrecv)
    lrecv[w] = lsend[...]

    wide_recv(6, mbr)
    total = sum_messages(mbr) / SAMPLES
    m1 = jnp.concatenate([total[q:q + 1] for q in range(4)], axis=1)
    m2 = jnp.concatenate([total[q + 4:q + 5] for q in range(4)], axis=1)
    inv = jnp.concatenate(inv_b, axis=1)
    grad = inv * (dB[...] - m1 - S_b[own, :].astype(F32) * m2)
    for i in range(NN):
        rbs[i] = jnp.concatenate(
            [grad[i * 8:i * 8 + 8, h * HB:(h + 1) * HB] for h in (0, 1)], axis=0).astype(BF16)
    narrow_a2a(7, rbs, rbr)
    rbr[n] = rbs[n]

    wide_recv(7, rar)
    for i in range(WN):
        for h in (0, 1):
            ga_ref[:, i * SLAB + h * HS:i * SLAB + (h + 1) * HS] = rar[i, h * 8:h * 8 + 8, :]
    wide_recv(8, lrecv)
    loss = jnp.sum(sum_messages(lrecv), keepdims=True) / FEATS
    loss_ref[...] = jnp.broadcast_to(loss, loss_ref.shape)
    narrow_recv(7, rbr)
    for i in range(NN):
        for h in (0, 1):
            gb_ref[:, i * BLK + h * HB:i * BLK + (h + 1) * HB] = rbr[i, h * 8:h * 8 + 8, :]

    wide_sent(0, xa.at[0])
    narrow_sent(0, xb.at[0])
    wide_sent(1, B3.at[0])
    narrow_sent(1, A3.at[0])
    wide_sent(2, xb2.at[0])
    narrow_sent(2, xa2.at[0])
    wide_sent(3, gas.at[0])
    narrow_sent(3, gbs.at[0])

    @pl.when(diag)
    def _():
        wide_sent(4, va)
        narrow_sent(4, vb)
    wide_sent(5, gball.at[0])
    narrow_sent(5, gaall.at[0])
    wide_sent(6, mbs)
    narrow_sent(6, mas)
    wide_sent(7, ras.at[0])
    narrow_sent(7, rbs.at[0])
    wide_sent(8, lsend)
    lax.fori_loop(0, tiles, lambda i, c: (corr_out(i).wait(), c)[1], 0)


def solution(mesh):
    WN, NN = mesh.shape["wide"], mesh.shape["narrow"]

    def on_device(view_a, view_b):
        rows, features = view_a.shape
        samples = rows * WN * NN
        BLK = features // NN
        SLAB = features // WN
        HB, HS, HN = BLK // 2, SLAB // 2, samples // 2
        V = pltpu.VMEM
        vmem = pl.BlockSpec(memory_space=pltpu.VMEM)
        corr, loss, ga, gb = pl.pallas_call(
            functools.partial(kernel, WN, NN, BLK, samples),
            out_shape=(
                jax.ShapeDtypeStruct((SLAB, BLK), BF16),
                jax.ShapeDtypeStruct((8, 128), F32),
                jax.ShapeDtypeStruct((rows, features), BF16),
                jax.ShapeDtypeStruct((rows, features), BF16),
            ),
            in_specs=[vmem, vmem],
            out_specs=(pl.BlockSpec(memory_space=pl.ANY), vmem, vmem, vmem),
            scratch_shapes=[
                V((WN, 16, HS), BF16), V((NN, 16, HB), BF16),
                V((WN, 16, HS), BF16), V((NN, 16, HB), BF16),
                V((NN, WN, 16, HS), BF16), V((WN, NN, 16, HB), BF16),
                V((WN, 16, HS), BF16), V((NN, 16, HB), BF16),
                V((samples, SLAB), BF16), V((samples, BLK), BF16), V((WN * 8, SLAB), BF16),
                V((WN, 16, HN), BF16), V((WN, 16, HN), BF16), V((NN, 16, HN), BF16),
                V((NN, 16, HN), BF16), V((NN, 16, HN), BF16), V((WN, 16, HN), BF16),
                V((8, BLK), F32), V((8, BLK), F32), V((8, BLK), F32), V((2, 8, BLK), F32),
                V((WN * 8, SLAB), F32), V((NN * 8, BLK), F32),
                V((16, SLAB // 4), F32), V((NN, 16, SLAB // 4), F32),
                V((8, BLK // 4), F32), V((WN, 8, BLK // 4), F32),
                V((WN, 16, HS), BF16), V((WN, 16, HS), BF16),
                V((NN, 16, HB), BF16), V((NN, 16, HB), BF16),
                V((8, BLK), F32), V((8, BLK // 2), F32), V((WN, 8, BLK // 2), F32),
                V((SLAB, BLK), BF16),
                pltpu.SemaphoreType.DMA((9, WN)), pltpu.SemaphoreType.DMA((9, WN)),
                pltpu.SemaphoreType.DMA((9, NN)), pltpu.SemaphoreType.DMA((9, NN)),
                pltpu.SemaphoreType.DMA((8,)),
            ],
            compiler_params=pltpu.CompilerParams(
                collective_id=0, has_side_effects=True, vmem_limit_bytes=56 * 1024 * 1024),
        )(view_a, view_b)
        return corr, loss[0, 0], ga, gb

    return jax.shard_map(
        on_device,
        mesh=mesh,
        in_specs=(P(("wide", "narrow"), None), P(("wide", "narrow"), None)),
        out_specs=(
            P("wide", "narrow"),
            P(),
            P(("wide", "narrow"), None),
            P(("wide", "narrow"), None),
        ),
        check_vma=False,
    )
```

```python
import functools

import jax
import jax.numpy as jnp
from jax import lax
from jax.experimental import pallas as pl
from jax.experimental.pallas import tpu as pltpu
from jax.sharding import PartitionSpec as P

off_weight = 0.0051
epsilon = 1e-05
MESH = pl.DeviceIdType.MESH
F32 = jnp.float32
BF16 = jnp.bfloat16


def kernel(
    WN, NN, BLK, SAMPLES,
    a_hbm, b_hbm,
    corr_ref, loss_ref, ga_ref, gb_ref,
    a_ref, b_ref, dummy,
    xa, xb, xb2, xa2,
    A3, B3, b1w, a1n,
    S_a, S_b, SR_a,
    gas, gar, gaall, gbs, gbr, gball,
    va, vb, Dn, Dw,
    dA, dB,
    mas, mar, mbs, mbr,
    ras, rar, rbs, rbr,
    lbuf, lsend, lrecv,
    s_w, r_w, s_n, r_n, r_a, r_b, r_d, in_sem,
):
    SLAB = BLK * (NN // WN)
    HB, HS = BLK // 2, SLAB // 2
    HN = SAMPLES // 2
    FEATS = BLK * NN
    w = lax.axis_index("wide")
    n = lax.axis_index("narrow")
    diag = lax.div(n, 2) == w

    def wide_copy(which, k, src, dst):
        return pltpu.make_async_remote_copy(
            src_ref=src, dst_ref=dst, send_sem=s_w.at[which], recv_sem=r_w.at[which],
            device_id=(lax.rem(w + k, WN), n), device_id_type=MESH,
        )

    def narrow_copy(which, k, src, dst):
        return pltpu.make_async_remote_copy(
            src_ref=src, dst_ref=dst, send_sem=s_n.at[which], recv_sem=r_n.at[which],
            device_id=(w, lax.rem(n + k, NN)), device_id_type=MESH,
        )

    def each(count, body):
        def step(k, c):
            body(k)
            return c
        lax.fori_loop(1, count, step, 0)


    def wide_recv(which, dst):
        ref = dst.at[pl.ds(0, WN - 1)]
        wide_copy(which, 1, ref, ref).wait_recv()

    def narrow_recv(which, dst):
        ref = dst.at[pl.ds(0, NN - 1)]
        narrow_copy(which, 1, ref, ref).wait_recv()

    def wide_sent(which, dst):
        ref = dst.at[pl.ds(0, WN - 1)]
        wide_copy(which, 1, ref, ref).wait_send()

    def narrow_sent(which, dst):
        ref = dst.at[pl.ds(0, NN - 1)]
        narrow_copy(which, 1, ref, ref).wait_send()

    def wide_a2a(which, src, dst):
        each(WN, lambda k: wide_copy(which, k, src.at[lax.rem(w + k, WN)], dst.at[w]).start())

    def narrow_a2a(which, src, dst):
        each(NN, lambda k: narrow_copy(which, k, src.at[lax.rem(n + k, NN)], dst.at[n]).start())

    def wide_bcast(which, src, dst):
        each(WN, lambda k: wide_copy(which, k, src, dst.at[w]).start())

    def narrow_bcast(which, src, dst):
        each(NN, lambda k: narrow_copy(which, k, src, dst.at[n]).start())

    loads = [
        pltpu.make_async_copy(a_hbm, a_ref, in_sem.at[0]),
        pltpu.make_async_copy(b_hbm, b_ref, in_sem.at[1]),
    ]
    for load in loads:
        load.start()
    barrier = pltpu.get_barrier_semaphore()
    each(WN, lambda k: pl.semaphore_signal(
        barrier, inc=1, device_id=(lax.rem(w + k, WN), n), device_id_type=MESH))
    each(NN, lambda k: pl.semaphore_signal(
        barrier, inc=1, device_id=(w, lax.rem(n + k, NN)), device_id_type=MESH))

    for load in loads:
        load.wait()

    def stack(ref, base, half):
        return jnp.concatenate(
            [ref[:, base:base + half], ref[:, base + half:base + 2 * half]], axis=0)

    for i in range(WN):
        xa[i] = stack(a_ref, i * SLAB, HS)
    for i in range(NN):
        xb[i] = stack(b_ref, i * BLK, HB)
    pl.semaphore_wait(barrier, WN + NN - 2)

    wide_a2a(0, xa, A3.at[n])
    narrow_a2a(0, xb, B3.at[w])
    A3[n, w] = xa[w]
    B3[w, n] = xb[n]
    for i in range(WN):
        xb2[i] = stack(b_ref, i * SLAB, HS)
    for i in range(NN):
        xa2[i] = stack(a_ref, i * BLK, HB)
    b1w[w] = xb2[w]
    a1n[n] = xa2[n]
    z, y = lax.div(n, 4), lax.rem(n, 4)
    x, core = lax.div(w, 2), lax.rem(w, 2)
    PART = WN // 2
    FULL, FIRST, SECOND = (0, PART), (0, PART // 2), (PART // 2, PART // 2)

    def slot(part, p, q):
        dz, dy = (q, p) if part == 0 else (p, q)
        return lax.rem(z + dz + 4, 4) * 4 + lax.rem(y + dy + 4, 4)

    def piece(part, at, cut):
        return A3.at[at, pl.ds(part * PART + cut[0], cut[1])]

    def move(part, index, at, cut, p, q):
        ref = piece(part, at, cut)
        return pltpu.make_async_remote_copy(
            src_ref=ref, dst_ref=ref, send_sem=s_n.at[1], recv_sem=r_a.at[part, index],
            device_id=(w, slot(part, p, q)), device_id_type=MESH,
        )

    LINES = (0, -1, 1, 2)

    def along(part, line, p, stage):
        step = (lambda d: (d, 0)) if stage == 1 else (lambda d: (0, d))
        for d, index in ((1, 0), (-1, 1)):
            move(part, line * 4 + index, slot(part, p, 0), FULL, *step(d)).start()

    def relay(part, line, p, stage):
        for d, index, cut in ((1, 2, FIRST), (-1, 3, SECOND)):
            got = slot(part, -d, 0) if stage == 1 else slot(part, p, -d)
            step = (d, 0) if stage == 1 else (0, d)
            move(part, line * 4 + index - 2, got, FULL, 0, 0).wait_recv()
            move(part, line * 4 + index, got, cut, *step).start()

    def far(part, line, p, stage):
        got = slot(part, 2, 0) if stage == 1 else slot(part, p, 2)
        for index, cut in ((2, FIRST), (3, SECOND)):
            move(part, line * 4 + index, got, cut, 0, 0).wait_recv()

    def move_b(index, at, dx, other):
        ref = B3.at[at]
        to = lax.rem(x + dx + 4, 4) * 2 + (1 - core if other else core)
        return pltpu.make_async_remote_copy(
            src_ref=ref, dst_ref=ref, send_sem=s_w.at[1], recv_sem=r_b.at[index],
            device_id=(to, n), device_id_type=MESH,
        )

    def slot_b(dx, other):
        return lax.rem(x + dx + 4, 4) * 2 + (1 - core if other else core)

    wide_recv(0, A3.at[n])
    for part in (0, 1):
        along(part, 4, 0, 1)
    for part in (0, 1):
        along(part, 0, 0, 2)
    narrow_recv(0, B3.at[w])
    for i, dx in enumerate((1, -1, 2)):
        move_b(i, w, dx, False).start()
    move_b(3, w, 0, True).start()
    wide_a2a(2, xb2, b1w)

    def add_sums(ref, sums):
        def step(i, c):
            v = ref[i].astype(F32)
            return (c[0] + v, c[1] + v * v)
        return lax.fori_loop(0, ref.shape[0], step, sums, unroll=min(4, ref.shape[0]))

    def moments_of(sums):
        total, squares = sums

        def fold(t):
            return [jnp.sum(t[h * 8:(h + 1) * 8], axis=0, keepdims=True) / SAMPLES for h in (0, 1)]
        means, seconds = fold(total), fold(squares)
        invs = [lax.rsqrt(q - m * m + epsilon) for q, m in zip(seconds, means)]
        return means, invs

    def stacked(halves):
        return jnp.concatenate([jnp.broadcast_to(h, (8, h.shape[1])) for h in halves], axis=0)

    zero_b, zero_a = jnp.zeros((16, HB), F32), jnp.zeros((16, HS), F32)
    sums_b = add_sums(B3.at[w], (zero_b, zero_b))
    sums_a = add_sums(A3.at[n], (zero_a, zero_a))
    for part in (0, 1):
        relay(part, 4, 0, 1)
    for part in (0, 1):
        for line in (1, 2):
            along(part, line, LINES[line], 2)

    def take_b(i, dx, sums):
        got = slot_b(-dx, False)
        move_b(i, got, 0, False).wait_recv()
        move_b(4 + i, got, 0, True).start()
        return add_sums(B3.at[got], sums)

    def sums_of_piece(part, at, sums):
        return add_sums(piece(part, at, FULL), sums)

    for part in (0, 1):
        for p in (-1, 1):
            sums_a = sums_of_piece(part, slot(part, p, 0), sums_a)
    for part in (0, 1):
        relay(part, 0, 0, 2)
    for part in (0, 1):
        far(part, 4, 0, 1)
        along(part, 3, 2, 2)
    for i, dx in ((0, 1), (1, -1)):
        sums_b = take_b(i, dx, sums_b)
    for part in (0, 1):
        for line in (1, 2):
            relay(part, line, LINES[line], 2)
    sums_b = take_b(2, 2, sums_b)
    for part in (0, 1):
        for q in (-1, 1):
            sums_a = sums_of_piece(part, slot(part, 0, q), sums_a)
            for p in (-1, 1):
                sums_a = sums_of_piece(part, slot(part, p, q), sums_a)
        sums_a = sums_of_piece(part, slot(part, 2, 0), sums_a)
    for i, dx in ((3, 0), (4, 1), (5, -1), (6, 2)):
        move_b(i, slot_b(-dx, True), 0, True).wait_recv()
        sums_b = add_sums(B3.at[slot_b(-dx, True)], sums_b)
    for part in (0, 1):
        relay(part, 3, 2, 2)
    mean_b, inv_b = moments_of(sums_b)
    mean2, inv2 = stacked(mean_b), stacked(inv_b)

    def norm_b(i, c):
        src, pair = lax.div(i, NN // 2), lax.rem(i, NN // 2)
        even = (B3[src, 2 * pair].astype(F32) - mean2) * inv2
        odd = (B3[src, 2 * pair + 1].astype(F32) - mean2) * inv2
        at = pl.ds(pl.multiple_of(i * 16, 16), 16)
        for h in (0, 1):
            S_b[at, h * HB:(h + 1) * HB] = jnp.concatenate(
                [even[h * 8:h * 8 + 8], odd[h * 8:h * 8 + 8]], axis=0).astype(BF16)
        return c
    lax.fori_loop(0, SAMPLES // 16, norm_b, 0, unroll=2)

    dot_last = functools.partial(
        lax.dot_general, dimension_numbers=(((1,), (1,)), ((), ())), preferred_element_type=F32)

    def stack_gram(dst, g):
        count = g.shape[0] // 8
        g3 = g.reshape(count, 8, SAMPLES)
        dst[...] = jnp.concatenate([g3[:, :, :HN], g3[:, :, HN:]], axis=1).astype(BF16)

    own_rows = S_b[pl.ds(pl.multiple_of(w * NN * 8, 16), NN * 8), :]
    stack_gram(gbs, dot_last(own_rows, S_b[...]))
    narrow_a2a(3, gbs, gbr)
    gbr[n] = gbs[n]

    for part in (0, 1):
        for q in (-1, 1):
            sums_a = sums_of_piece(part, slot(part, 2, q), sums_a)
    for line in range(4):
        for part in (0, 1):
            far(part, line, LINES[line], 2)
            sums_a = sums_of_piece(part, slot(part, LINES[line], 2), sums_a)
    narrow_a2a(2, xa2, a1n)
    mean_a, inv_a = moments_of(sums_a)
    mean2a, inv2a = stacked(mean_a), stacked(inv_a)

    def norm_a(i, c):
        src, pair = lax.div(i, NN // 2), lax.rem(i, NN // 2)
        even = (A3[2 * pair, src].astype(F32) - mean2a) * inv2a
        odd = (A3[2 * pair + 1, src].astype(F32) - mean2a) * inv2a
        at = pl.ds(pl.multiple_of(i * 16, 16), 16)
        for h in (0, 1):
            S_a[at, h * HS:(h + 1) * HS] = jnp.concatenate(
                [even[h * 8:h * 8 + 8], odd[h * 8:h * 8 + 8]], axis=0).astype(BF16)
        return c
    lax.fori_loop(0, SAMPLES // 16, norm_a, 0)
    for i in range(WN // 2):
        even = (A3[n, 2 * i].astype(F32) - mean2a) * inv2a
        odd = (A3[n, 2 * i + 1].astype(F32) - mean2a) * inv2a
        for h in (0, 1):
            SR_a[i * 16:i * 16 + 16, h * HS:(h + 1) * HS] = jnp.concatenate(
                [even[h * 8:h * 8 + 8], odd[h * 8:h * 8 + 8]], axis=0).astype(BF16)

    stack_gram(gas, dot_last(SR_a[...], S_a[...]))
    wide_a2a(3, gas, gar)
    gar[w] = gas[w]

    half = lax.rem(n, 2)
    lbuf[...] = jnp.zeros_like(lbuf)

    def narrow_vec(k, h=None):
        h = half if h is None else h
        return pltpu.make_async_remote_copy(
            src_ref=vb, dst_ref=Dw.at[h], send_sem=s_n.at[4], recv_sem=r_d.at[h],
            device_id=(w, lax.rem(n + k, NN)), device_id_type=MESH,
        )

    @pl.when(diag)
    def _():
        def step(i, c):
            at = pl.ds(pl.multiple_of(i * 16, 16), 16)
            cols = pl.ds(pl.multiple_of(half * BLK, BLK), BLK)
            return c + S_a[at, cols].astype(F32) * S_b[at, :].astype(F32)
        prod = lax.fori_loop(0, SAMPLES // 16, step, jnp.zeros((16, BLK), F32), unroll=4)
        c = jnp.sum(prod, axis=0, keepdims=True) / SAMPLES
        d = -2.0 * (1.0 - c) - 2.0 * off_weight * c
        mb = jnp.concatenate(mean_b, axis=1)
        ib = jnp.concatenate(inv_b, axis=1)
        first = (half == 0).astype(F32)
        ma = mean_a[0] * first + mean_a[1] * (1.0 - first)
        ia = inv_a[0] * first + inv_a[1] * (1.0 - first)
        pad = jnp.zeros((5, BLK), F32)
        va[...] = jnp.concatenate([ma, ia, d, pad], axis=0)
        vb[...] = jnp.concatenate([mb, ib, d, pad], axis=0)
        Dn[...] = va[...]
        Dw[half] = vb[...]
        lbuf[0:1, :] = (1.0 - c) * (1.0 - c) - off_weight * c * c
        each(WN, lambda k: wide_copy(4, k, va, Dn).start())
        each(NN, lambda k: narrow_vec(k).start())

    def diag_recv():
        @pl.when(lax.div(n, 2) != w)
        def _():
            wide_copy(4, 1, va, Dn).wait_recv()
        for h in (0, 1):
            @pl.when(n != 2 * w + h)
            def _():
                narrow_vec(1, h).wait_recv()

    def diag_sent():
        @pl.when(diag)
        def _():
            ref = dummy.at[pl.ds(0, WN - 1)]
            wide_copy(4, 1, ref, ref).wait_send()
            ref = dummy.at[pl.ds(0, NN - 1)]
            narrow_copy(4, 1, ref, ref).wait_send()

    narrow_recv(3, gbr)

    def total_of(ref):
        t = ref[0].astype(F32)
        for i in range(1, ref.shape[0]):
            t = t + ref[i].astype(F32)
        return t
    gball[w] = total_of(gbr).astype(BF16)
    wide_bcast(5, gball.at[w], gball)

    TM = 256 if SLAB % 256 == 0 else SLAB

    def cross_tile(i, acc):
        at = pl.ds(pl.multiple_of(i * TM, TM), TM)
        c = lax.dot_general(
            S_a[:, at], S_b[...], (((0,), (0,)), ((), ())), preferred_element_type=F32
        ) * (1.0 / SAMPLES)
        corr_ref[at, :] = c.astype(BF16)
        return acc + jnp.sum((c * c).reshape(TM // 8, 8, BLK), axis=0)
    tiles = SLAB // TM
    acc = lax.fori_loop(0, 1, cross_tile, jnp.zeros((8, BLK), F32))

    wide_recv(3, gar)
    gaall[n] = total_of(gar).astype(BF16)
    narrow_bcast(5, gaall.at[n], gaall)
    acc = lax.fori_loop(1, tiles, cross_tile, acc)
    lbuf[...] = lbuf[...] + off_weight * acc

    wide_recv(2, b1w)
    narrow_recv(2, a1n)

    diag_recv()

    dmean, dinv, dd = (stacked([Dw[h, i:i + 1, :] for h in (0, 1)]) for i in range(3))
    for i in range(WN):
        s = ((b1w[i].astype(F32) - dmean) * dinv).astype(BF16).astype(F32) * dd
        for h in (0, 1):
            dA[i * 8:i * 8 + 8, h * HS:(h + 1) * HS] = s[h * 8:h * 8 + 8]
    dmean, dinv, dd = (
        stacked([Dn[i:i + 1, h * HB:(h + 1) * HB] for h in (0, 1)]) for i in range(3))
    for i in range(NN):
        s = ((a1n[i].astype(F32) - dmean) * dinv).astype(BF16).astype(F32) * dd
        for h in (0, 1):
            dB[i * 8:i * 8 + 8, h * HB:(h + 1) * HB] = s[h * 8:h * 8 + 8]

    factor = 2.0 * off_weight / SAMPLES

    def unstack(ref):
        g = ref[...].astype(F32)
        rows = ref.shape[0] * 8
        return [g[:, h * 8:h * 8 + 8, :].reshape(rows, HN).astype(BF16) for h in (0, 1)]

    def sum_messages(ref):
        t = ref[0]
        for i in range(1, ref.shape[0]):
            t = t + ref[i]
        return t

    wide_recv(5, gball)
    g0, g1 = unstack(gball)
    Q = SLAB // 4
    d = factor * (
        jnp.dot(g0, S_a[:HN, :], preferred_element_type=F32)
        + jnp.dot(g1, S_a[HN:, :], preferred_element_type=F32)
    ) + dA[...]
    dA[...] = d
    m1 = jnp.sum(d, axis=0, keepdims=True)
    m2 = jnp.sum(d * SR_a[...].astype(F32), axis=0, keepdims=True)
    mas[0:8, :] = jnp.concatenate(
        [m[:, q * Q:(q + 1) * Q] for m in (m1, m2) for q in range(4)], axis=0)
    mas[8:16, :] = lbuf[:, :BLK // 2] + lbuf[:, BLK // 2:]
    narrow_bcast(6, mas, mar)
    mar[n] = mas[...]

    narrow_recv(5, gaall)
    g0, g1 = unstack(gaall)
    own = pl.ds(pl.multiple_of(w * NN * 8, 16), NN * 8)
    d = factor * (
        jnp.dot(g0, S_b[:HN, :], preferred_element_type=F32)
        + jnp.dot(g1, S_b[HN:, :], preferred_element_type=F32)
    ) + dB[...]
    dB[...] = d
    m1 = jnp.sum(d, axis=0, keepdims=True)
    m2 = jnp.sum(d * S_b[own, :].astype(F32), axis=0, keepdims=True)
    QB = BLK // 4
    mbs[...] = jnp.concatenate(
        [m[:, q * QB:(q + 1) * QB] for m in (m1, m2) for q in range(4)], axis=0)
    wide_bcast(6, mbs, mbr)
    mbr[w] = mbs[...]

    narrow_recv(6, mar)
    total = sum_messages(mar) / SAMPLES
    m1 = jnp.concatenate([total[q:q + 1] for q in range(4)], axis=1)
    m2 = jnp.concatenate([total[q + 4:q + 5] for q in range(4)], axis=1)
    inv = jnp.concatenate(inv_a, axis=1)
    grad = inv * (dA[...] - m1 - SR_a[...].astype(F32) * m2)
    for i in range(WN):
        ras[i] = jnp.concatenate(
            [grad[i * 8:i * 8 + 8, h * HS:(h + 1) * HS] for h in (0, 1)], axis=0).astype(BF16)
    wide_a2a(7, ras, rar)
    rar[w] = ras[w]
    lsend[...] = total[8:16] * SAMPLES
    wide_bcast(8, lsend, lrecv)
    lrecv[w] = lsend[...]

    wide_recv(6, mbr)
    total = sum_messages(mbr) / SAMPLES
    m1 = jnp.concatenate([total[q:q + 1] for q in range(4)], axis=1)
    m2 = jnp.concatenate([total[q + 4:q + 5] for q in range(4)], axis=1)
    inv = jnp.concatenate(inv_b, axis=1)
    grad = inv * (dB[...] - m1 - S_b[own, :].astype(F32) * m2)
    for i in range(NN):
        rbs[i] = jnp.concatenate(
            [grad[i * 8:i * 8 + 8, h * HB:(h + 1) * HB] for h in (0, 1)], axis=0).astype(BF16)
    narrow_a2a(7, rbs, rbr)
    rbr[n] = rbs[n]

    wide_recv(7, rar)
    for i in range(WN):
        for h in (0, 1):
            ga_ref[:, i * SLAB + h * HS:i * SLAB + (h + 1) * HS] = rar[i, h * 8:h * 8 + 8, :]
    wide_recv(8, lrecv)
    loss_ref[...] = sum_messages(lrecv) / FEATS
    narrow_recv(7, rbr)
    for i in range(NN):
        for h in (0, 1):
            gb_ref[:, i * BLK + h * HB:i * BLK + (h + 1) * HB] = rbr[i, h * 8:h * 8 + 8, :]

    wide_sent(0, A3.at[n])
    narrow_sent(0, B3.at[w])
    wide_sent(1, B3)
    narrow_sent(1, A3)
    wide_sent(2, b1w)
    narrow_sent(2, a1n)
    wide_sent(3, gar)
    narrow_sent(3, gbr)
    diag_sent()
    wide_sent(5, gball)
    narrow_sent(5, gaall)
    wide_sent(6, mbr)
    narrow_sent(6, mar)
    wide_sent(7, rar)
    narrow_sent(7, rbr)
    wide_sent(8, lrecv)


def write_out(corr, loss, ga, gb, corr_out, loss_out, ga_out, gb_out, sem):
    rows = corr.shape[0] // 8
    copies = [
        pltpu.make_async_copy(
            corr.at[pl.ds(i * rows, rows)], corr_out.at[pl.ds(i * rows, rows)], sem.at[i])
        for i in range(8)
    ]
    copies.append(pltpu.make_async_copy(ga, ga_out, sem.at[8]))
    copies.append(pltpu.make_async_copy(gb, gb_out, sem.at[9]))
    for copy in copies:
        copy.start()
    loss_out[0, 0] = jnp.sum(loss[...])
    for copy in copies:
        copy.wait()


def solution(mesh):
    WN, NN = mesh.shape["wide"], mesh.shape["narrow"]

    def on_device(view_a, view_b):
        rows, features = view_a.shape
        samples = rows * WN * NN
        BLK = features // NN
        SLAB = features // WN
        HB, HS, HN = BLK // 2, SLAB // 2, samples // 2
        V = pltpu.VMEM
        vmem = pl.BlockSpec(memory_space=pltpu.VMEM)
        hbm = pl.BlockSpec(memory_space=pltpu.HBM)
        anywhere = pl.BlockSpec(memory_space=pl.ANY)
        dma = pltpu.SemaphoreType.DMA
        corr, loss, ga, gb = pl.pallas_call(
            functools.partial(kernel, WN, NN, BLK, samples),
            out_shape=(
                V((SLAB, BLK), BF16),
                V((8, BLK // 2), F32),
                V((rows, features), BF16),
                V((rows, features), BF16),
            ),
            in_specs=[hbm, hbm],
            out_specs=(vmem, vmem, vmem, vmem),
            scratch_shapes=[
                V((rows, features), BF16), V((rows, features), BF16), V((NN, 8, BLK), F32),
                V((WN, 16, HS), BF16), V((NN, 16, HB), BF16),
                V((WN, 16, HS), BF16), V((NN, 16, HB), BF16),
                V((NN, WN, 16, HS), BF16), V((WN, NN, 16, HB), BF16),
                V((WN, 16, HS), BF16), V((NN, 16, HB), BF16),
                V((samples, SLAB), BF16), V((samples, BLK), BF16), V((WN * 8, SLAB), BF16),
                V((WN, 16, HN), BF16), V((WN, 16, HN), BF16), V((NN, 16, HN), BF16),
                V((NN, 16, HN), BF16), V((NN, 16, HN), BF16), V((WN, 16, HN), BF16),
                V((8, BLK), F32), V((8, BLK), F32), V((8, BLK), F32), V((2, 8, BLK), F32),
                V((WN * 8, SLAB), F32), V((NN * 8, BLK), F32),
                V((16, SLAB // 4), F32), V((NN, 16, SLAB // 4), F32),
                V((8, BLK // 4), F32), V((WN, 8, BLK // 4), F32),
                V((WN, 16, HS), BF16), V((WN, 16, HS), BF16),
                V((NN, 16, HB), BF16), V((NN, 16, HB), BF16),
                V((8, BLK), F32), V((8, BLK // 2), F32), V((WN, 8, BLK // 2), F32),
                dma((9,)), dma((9,)), dma((9,)), dma((9,)),
                dma((2, 20)), dma((7,)), dma((2,)), dma((2,)),
            ],
            compiler_params=pltpu.CompilerParams(
                collective_id=0, has_side_effects=True, vmem_limit_bytes=32 * 1024 * 1024),
        )(*(pltpu.with_memory_space_constraint(v, pltpu.HBM) for v in (view_a, view_b)))
        corr, loss, ga, gb = pl.pallas_call(
            write_out,
            out_shape=(
                jax.ShapeDtypeStruct((SLAB, BLK), BF16),
                jax.ShapeDtypeStruct((1, 1), F32),
                jax.ShapeDtypeStruct((rows, features), BF16),
                jax.ShapeDtypeStruct((rows, features), BF16),
            ),
            in_specs=[anywhere, vmem, anywhere, anywhere],
            out_specs=(anywhere, pl.BlockSpec(memory_space=pltpu.SMEM), anywhere, anywhere),
            scratch_shapes=[dma((10,))],
            compiler_params=pltpu.CompilerParams(vmem_limit_bytes=8 * 1024 * 1024),
        )(corr, loss, ga, gb)
        return corr, loss.reshape(()), ga, gb

    return jax.shard_map(
        on_device,
        mesh=mesh,
        in_specs=(P(("wide", "narrow"), None), P(("wide", "narrow"), None)),
        out_specs=(
            P("wide", "narrow"),
            P(),
            P(("wide", "narrow"), None),
            P(("wide", "narrow"), None),
        ),
        check_vma=False,
    )
```

```python
import functools

import jax
import jax.numpy as jnp
from jax import lax
from jax.experimental import pallas as pl
from jax.experimental.pallas import tpu as pltpu
from jax.sharding import PartitionSpec as P

off_weight = 0.0051
epsilon = 1e-05
MESH = pl.DeviceIdType.MESH
F32 = jnp.float32
BF16 = jnp.bfloat16


def kernel(
    WN, NN, BLK, SAMPLES,
    a_hbm, b_hbm,
    corr_ref, loss_ref, ga_ref, gb_ref,
    a_ref, b_ref, dummy,
    xa, xb, xb2, xa2,
    A3, B3, b1w, a1n,
    S_a, S_b, SR_a,
    gas, gar, gaall, gbs, gbr, gball,
    va, vb, Dn, Dw,
    dA, dB,
    mas, mar, mbs, mbr, ea, eb,
    ras, rar, rbs, rbr,
    lbuf, lsend, lrecv,
    s_w, r_w, s_n, r_n, r_a, r_b, r_d, in_sem,
):
    SLAB = BLK * (NN // WN)
    HB, HS = BLK // 2, SLAB // 2
    HN = SAMPLES // 2
    FEATS = BLK * NN
    w = lax.axis_index("wide")
    n = lax.axis_index("narrow")
    diag = lax.div(n, 2) == w

    z, y = lax.div(n, 4), lax.rem(n, 4)
    x, core = lax.div(w, 2), lax.rem(w, 2)

    def offset(j):
        return lax.rem(2 + 3 * j + 3 * lax.div(j * (j - 1), 2), 4)

    def wide_peer(i):
        return lax.rem(x + offset(lax.div(i, 2)), 4) * 2 + lax.rem(core + 1 - lax.rem(i, 2), 2)

    def narrow_peer(i):
        return lax.rem(z + offset(lax.div(i, 4)), 4) * 4 + lax.rem(y + offset(lax.rem(i, 4)), 4)

    def wide_copy(which, k, src, dst):
        return pltpu.make_async_remote_copy(
            src_ref=src, dst_ref=dst, send_sem=s_w.at[which], recv_sem=r_w.at[which],
            device_id=(wide_peer(k), n), device_id_type=MESH,
        )

    def narrow_copy(which, k, src, dst):
        return pltpu.make_async_remote_copy(
            src_ref=src, dst_ref=dst, send_sem=s_n.at[which], recv_sem=r_n.at[which],
            device_id=(w, narrow_peer(k)), device_id_type=MESH,
        )

    def each(count, body):
        def step(k, c):
            body(k)
            return c
        lax.fori_loop(0, count - 1, step, 0)


    def wide_recv(which, dst):
        ref = dst.at[pl.ds(0, WN - 1)]
        wide_copy(which, 1, ref, ref).wait_recv()

    def narrow_recv(which, dst):
        ref = dst.at[pl.ds(0, NN - 1)]
        narrow_copy(which, 1, ref, ref).wait_recv()

    def wide_sent(which, dst):
        ref = dst.at[pl.ds(0, WN - 1)]
        wide_copy(which, 1, ref, ref).wait_send()

    def narrow_sent(which, dst):
        ref = dst.at[pl.ds(0, NN - 1)]
        narrow_copy(which, 1, ref, ref).wait_send()

    def wide_a2a(which, src, dst):
        each(WN, lambda k: wide_copy(which, k, src.at[wide_peer(k)], dst.at[w]).start())

    def narrow_a2a(which, src, dst):
        each(NN, lambda k: narrow_copy(which, k, src.at[narrow_peer(k)], dst.at[n]).start())

    def wide_bcast(which, src, dst):
        each(WN, lambda k: wide_copy(which, k, src, dst.at[w]).start())

    def narrow_bcast(which, src, dst):
        each(NN, lambda k: narrow_copy(which, k, src, dst.at[n]).start())

    loads = [
        pltpu.make_async_copy(a_hbm, a_ref, in_sem.at[0]),
        pltpu.make_async_copy(b_hbm, b_ref, in_sem.at[1]),
    ]
    for load in loads:
        load.start()
    barrier = pltpu.get_barrier_semaphore()
    each(WN, lambda k: pl.semaphore_signal(
        barrier, inc=1, device_id=(wide_peer(k), n), device_id_type=MESH))
    each(NN, lambda k: pl.semaphore_signal(
        barrier, inc=1, device_id=(w, narrow_peer(k)), device_id_type=MESH))

    for load in loads:
        load.wait()

    def stack(ref, base, half):
        return jnp.concatenate(
            [ref[:, base:base + half], ref[:, base + half:base + 2 * half]], axis=0)

    for i in range(WN):
        xa[i] = stack(a_ref, i * SLAB, HS)
    for i in range(NN):
        xb[i] = stack(b_ref, i * BLK, HB)
    pl.semaphore_wait(barrier, WN + NN - 2)

    wide_a2a(0, xa, A3.at[n])
    narrow_a2a(0, xb, B3.at[w])
    A3[n, w] = xa[w]
    B3[w, n] = xb[n]
    for i in range(WN):
        xb2[i] = stack(b_ref, i * SLAB, HS)
    for i in range(NN):
        xa2[i] = stack(a_ref, i * BLK, HB)
    b1w[w] = xb2[w]
    a1n[n] = xa2[n]
    PART = WN // 2
    FULL, FIRST, SECOND = (0, PART), (0, PART // 2), (PART // 2, PART // 2)

    def slot(part, p, q):
        dz, dy = (q, p) if part == 0 else (p, q)
        return lax.rem(z + dz + 4, 4) * 4 + lax.rem(y + dy + 4, 4)

    def piece(part, at, cut):
        return A3.at[at, pl.ds(part * PART + cut[0], cut[1])]

    def move(part, index, at, cut, p, q):
        ref = piece(part, at, cut)
        return pltpu.make_async_remote_copy(
            src_ref=ref, dst_ref=ref, send_sem=s_n.at[1], recv_sem=r_a.at[part, index],
            device_id=(w, slot(part, p, q)), device_id_type=MESH,
        )

    LINES = (0, -1, 1, 2)

    def along(part, line, p, stage):
        step = (lambda d: (d, 0)) if stage == 1 else (lambda d: (0, d))
        for d, index in ((1, 0), (-1, 1)):
            move(part, line * 4 + index, slot(part, p, 0), FULL, *step(d)).start()

    def relay(part, line, p, stage):
        for d, index, cut in ((1, 2, FIRST), (-1, 3, SECOND)):
            got = slot(part, -d, 0) if stage == 1 else slot(part, p, -d)
            step = (d, 0) if stage == 1 else (0, d)
            move(part, line * 4 + index - 2, got, FULL, 0, 0).wait_recv()
            move(part, line * 4 + index, got, cut, *step).start()

    def far(part, line, p, stage):
        got = slot(part, 2, 0) if stage == 1 else slot(part, p, 2)
        for index, cut in ((2, FIRST), (3, SECOND)):
            move(part, line * 4 + index, got, cut, 0, 0).wait_recv()

    def move_b(index, at, dx, other):
        ref = B3.at[at]
        to = lax.rem(x + dx + 4, 4) * 2 + (1 - core if other else core)
        return pltpu.make_async_remote_copy(
            src_ref=ref, dst_ref=ref, send_sem=s_w.at[1], recv_sem=r_b.at[index],
            device_id=(to, n), device_id_type=MESH,
        )

    def slot_b(dx, other):
        return lax.rem(x + dx + 4, 4) * 2 + (1 - core if other else core)

    wide_recv(0, A3.at[n])
    for part in (0, 1):
        along(part, 4, 0, 1)
    for part in (0, 1):
        along(part, 0, 0, 2)
    narrow_recv(0, B3.at[w])
    for i, dx in enumerate((1, -1, 2)):
        move_b(i, w, dx, False).start()
    move_b(3, w, 0, True).start()
    wide_a2a(2, xb2, b1w)

    def add_sums(ref, sums):
        def step(i, c):
            v = ref[i].astype(F32)
            return (c[0] + v, c[1] + v * v)
        return lax.fori_loop(0, ref.shape[0], step, sums, unroll=min(4, ref.shape[0]))

    def moments_of(sums):
        total, squares = sums

        def fold(t):
            return [jnp.sum(t[h * 8:(h + 1) * 8], axis=0, keepdims=True) / SAMPLES for h in (0, 1)]
        means, seconds = fold(total), fold(squares)
        invs = [lax.rsqrt(q - m * m + epsilon) for q, m in zip(seconds, means)]
        return means, invs

    def stacked(halves):
        return jnp.concatenate([jnp.broadcast_to(h, (8, h.shape[1])) for h in halves], axis=0)

    zero_b, zero_a = jnp.zeros((16, HB), F32), jnp.zeros((16, HS), F32)
    sums_b = add_sums(B3.at[w], (zero_b, zero_b))
    sums_a = add_sums(A3.at[n], (zero_a, zero_a))
    for part in (0, 1):
        relay(part, 4, 0, 1)
    for part in (0, 1):
        for line in (1, 2):
            along(part, line, LINES[line], 2)

    def take_b(i, dx, sums):
        got = slot_b(-dx, False)
        move_b(i, got, 0, False).wait_recv()
        move_b(4 + i, got, 0, True).start()
        return add_sums(B3.at[got], sums)

    def sums_of_piece(part, at, sums):
        return add_sums(piece(part, at, FULL), sums)

    for part in (0, 1):
        for p in (-1, 1):
            sums_a = sums_of_piece(part, slot(part, p, 0), sums_a)
    for part in (0, 1):
        relay(part, 0, 0, 2)
    for part in (0, 1):
        far(part, 4, 0, 1)
        along(part, 3, 2, 2)
    for i, dx in ((0, 1), (1, -1)):
        sums_b = take_b(i, dx, sums_b)
    for part in (0, 1):
        for line in (1, 2):
            relay(part, line, LINES[line], 2)
    sums_b = take_b(2, 2, sums_b)
    for part in (0, 1):
        for q in (-1, 1):
            sums_a = sums_of_piece(part, slot(part, 0, q), sums_a)
            for p in (-1, 1):
                sums_a = sums_of_piece(part, slot(part, p, q), sums_a)
        sums_a = sums_of_piece(part, slot(part, 2, 0), sums_a)
    for i, dx in ((3, 0), (4, 1), (5, -1), (6, 2)):
        move_b(i, slot_b(-dx, True), 0, True).wait_recv()
        sums_b = add_sums(B3.at[slot_b(-dx, True)], sums_b)
    for part in (0, 1):
        relay(part, 3, 2, 2)
    mean_b, inv_b = moments_of(sums_b)
    mean2, inv2 = stacked(mean_b), stacked(inv_b)

    def norm_b(i, c):
        src, pair = lax.div(i, NN // 2), lax.rem(i, NN // 2)
        even = (B3[src, 2 * pair].astype(F32) - mean2) * inv2
        odd = (B3[src, 2 * pair + 1].astype(F32) - mean2) * inv2
        at = pl.ds(pl.multiple_of(i * 16, 16), 16)
        for h in (0, 1):
            S_b[at, h * HB:(h + 1) * HB] = jnp.concatenate(
                [even[h * 8:h * 8 + 8], odd[h * 8:h * 8 + 8]], axis=0).astype(BF16)
        return c
    lax.fori_loop(0, SAMPLES // 16, norm_b, 0, unroll=2)

    dot_last = functools.partial(
        lax.dot_general, dimension_numbers=(((1,), (1,)), ((), ())), preferred_element_type=F32)

    def stack_gram(dst, g):
        count = g.shape[0] // 8
        g3 = g.reshape(count, 8, SAMPLES)
        dst[...] = jnp.concatenate([g3[:, :, :HN], g3[:, :, HN:]], axis=1).astype(BF16)

    own_rows = S_b[pl.ds(pl.multiple_of(w * NN * 8, 16), NN * 8), :]
    stack_gram(gbs, dot_last(own_rows, S_b[...]))
    narrow_a2a(3, gbs, gbr)
    gbr[n] = gbs[n]

    for part in (0, 1):
        for q in (-1, 1):
            sums_a = sums_of_piece(part, slot(part, 2, q), sums_a)
    for line in range(4):
        for part in (0, 1):
            far(part, line, LINES[line], 2)
            sums_a = sums_of_piece(part, slot(part, LINES[line], 2), sums_a)
    mean_a, inv_a = moments_of(sums_a)
    mean2a, inv2a = stacked(mean_a), stacked(inv_a)

    def norm_a(i, c):
        src, pair = lax.div(i, NN // 2), lax.rem(i, NN // 2)
        even = (A3[2 * pair, src].astype(F32) - mean2a) * inv2a
        odd = (A3[2 * pair + 1, src].astype(F32) - mean2a) * inv2a
        at = pl.ds(pl.multiple_of(i * 16, 16), 16)
        for h in (0, 1):
            S_a[at, h * HS:(h + 1) * HS] = jnp.concatenate(
                [even[h * 8:h * 8 + 8], odd[h * 8:h * 8 + 8]], axis=0).astype(BF16)
        return c
    lax.fori_loop(0, SAMPLES // 16, norm_a, 0)
    for i in range(WN // 2):
        even = (A3[n, 2 * i].astype(F32) - mean2a) * inv2a
        odd = (A3[n, 2 * i + 1].astype(F32) - mean2a) * inv2a
        for h in (0, 1):
            SR_a[i * 16:i * 16 + 16, h * HS:(h + 1) * HS] = jnp.concatenate(
                [even[h * 8:h * 8 + 8], odd[h * 8:h * 8 + 8]], axis=0).astype(BF16)

    stack_gram(gas, dot_last(SR_a[...], S_a[...]))
    wide_a2a(3, gas, gar)
    gar[w] = gas[w]

    narrow_a2a(2, xa2, a1n)
    ones = jnp.ones((8, SAMPLES), BF16)
    mstd_a = jnp.dot(ones, S_a[...], preferred_element_type=F32) / SAMPLES
    mstd_b = jnp.dot(ones, S_b[...], preferred_element_type=F32) / SAMPLES

    half = lax.rem(n, 2)
    lbuf[...] = jnp.zeros_like(lbuf)
    ea[...] = jnp.zeros_like(ea)
    eb[...] = jnp.zeros_like(eb)

    def narrow_vec(k, h=None):
        h = half if h is None else h
        return pltpu.make_async_remote_copy(
            src_ref=vb, dst_ref=Dw.at[h], send_sem=s_n.at[4], recv_sem=r_d.at[h],
            device_id=(w, narrow_peer(k)), device_id_type=MESH,
        )

    @pl.when(diag)
    def _():
        def step(i, c):
            at = pl.ds(pl.multiple_of(i * 16, 16), 16)
            cols = pl.ds(pl.multiple_of(half * BLK, BLK), BLK)
            return c + S_a[at, cols].astype(F32) * S_b[at, :].astype(F32)
        prod = lax.fori_loop(0, SAMPLES // 16, step, jnp.zeros((16, BLK), F32), unroll=4)
        c = jnp.sum(prod, axis=0, keepdims=True) / SAMPLES
        d = -2.0 * (1.0 - c) - 2.0 * off_weight * c
        mb = jnp.concatenate(mean_b, axis=1)
        ib = jnp.concatenate(inv_b, axis=1)
        first = (half == 0).astype(F32)
        ma = mean_a[0] * first + mean_a[1] * (1.0 - first)
        ia = inv_a[0] * first + inv_a[1] * (1.0 - first)
        msa = mstd_a[0:1, :BLK] * first + mstd_a[0:1, BLK:] * (1.0 - first)
        pad = jnp.zeros((6, BLK), F32)
        ea[half] = jnp.concatenate([d * mstd_b[0:1], d * c, pad], axis=0)
        eb[...] = jnp.concatenate([d * msa, d * c, pad], axis=0)
        pad = jnp.zeros((5, BLK), F32)
        va[...] = jnp.concatenate([ma, ia, d, pad], axis=0)
        vb[...] = jnp.concatenate([mb, ib, d, pad], axis=0)
        Dn[...] = va[...]
        Dw[half] = vb[...]
        lbuf[0:1, :] = (1.0 - c) * (1.0 - c) - off_weight * c * c
        each(WN, lambda k: wide_copy(4, k, va, Dn).start())
        each(NN, lambda k: narrow_vec(k).start())

    def diag_recv():
        @pl.when(lax.div(n, 2) != w)
        def _():
            wide_copy(4, 1, va, Dn).wait_recv()
        for h in (0, 1):
            @pl.when(n != 2 * w + h)
            def _():
                narrow_vec(1, h).wait_recv()

    def diag_sent():
        @pl.when(diag)
        def _():
            ref = dummy.at[pl.ds(0, WN - 1)]
            wide_copy(4, 1, ref, ref).wait_send()
            ref = dummy.at[pl.ds(0, NN - 1)]
            narrow_copy(4, 1, ref, ref).wait_send()

    TM = SLAB // 2
    acc = jnp.zeros((8, BLK), F32)
    fb = jnp.zeros((8, BLK), F32)
    ones = jnp.ones((8, BLK), BF16)
    msb = mstd_b.astype(BF16)
    fa, sa = [], []
    for t in range(2):
        at = slice(t * TM, (t + 1) * TM)
        c = lax.dot_general(
            S_a[:, at], S_b[...], (((0,), (0,)), ((), ())), preferred_element_type=F32
        ) * (1.0 / SAMPLES)
        rounded = c.astype(BF16)
        corr_ref[at, :] = rounded
        squares = c * c
        acc = acc + jnp.sum(squares.reshape(TM // 8, 8, BLK), axis=0)
        fa.append(dot_last(msb, rounded)[0:1])
        sa.append(dot_last(ones, squares.astype(BF16))[0:1])
        fb = fb + jnp.dot(mstd_a[:, at].astype(BF16), rounded, preferred_element_type=F32)
    twice = 2.0 * off_weight
    m1 = jnp.concatenate([twice * fa[h] + ea[h, 0:1] for h in (0, 1)], axis=1)
    m2 = jnp.concatenate([twice * sa[h] + ea[h, 1:2] for h in (0, 1)], axis=1)
    Q = SLAB // 4
    lost = lbuf[...] + off_weight * acc
    mas[...] = jnp.concatenate(
        [jnp.concatenate([m[:, q * Q:(q + 1) * Q] for m in (m1, m2) for q in range(4)], axis=0)]
        + [sum(lost[:, q * 128:(q + 1) * 128] for q in range(BLK // 128))], axis=1)
    narrow_bcast(6, mas, mar)
    mar[n] = mas[...]
    m1 = twice * fb[0:1] + eb[0:1]
    m2 = twice * jnp.sum(acc, axis=0, keepdims=True) + eb[1:2]
    QB = BLK // 4
    mbs[...] = jnp.concatenate(
        [m[:, q * QB:(q + 1) * QB] for m in (m1, m2) for q in range(4)], axis=0)
    wide_bcast(6, mbs, mbr)
    mbr[w] = mbs[...]

    def total_of(ref):
        t = ref[0].astype(F32)
        for i in range(1, ref.shape[0]):
            t = t + ref[i].astype(F32)
        return t
    wide_recv(3, gar)
    gaall[n] = total_of(gar).astype(BF16)
    narrow_bcast(5, gaall.at[n], gaall)
    narrow_recv(3, gbr)
    gball[w] = total_of(gbr).astype(BF16)
    wide_bcast(5, gball.at[w], gball)

    wide_recv(2, b1w)
    narrow_recv(2, a1n)

    diag_recv()

    dmean, dinv, dd = (stacked([Dw[h, i:i + 1, :] for h in (0, 1)]) for i in range(3))
    for i in range(WN):
        s = ((b1w[i].astype(F32) - dmean) * dinv).astype(BF16).astype(F32) * dd
        for h in (0, 1):
            dA[i * 8:i * 8 + 8, h * HS:(h + 1) * HS] = s[h * 8:h * 8 + 8]
    dmean, dinv, dd = (
        stacked([Dn[i:i + 1, h * HB:(h + 1) * HB] for h in (0, 1)]) for i in range(3))
    for i in range(NN):
        s = ((a1n[i].astype(F32) - dmean) * dinv).astype(BF16).astype(F32) * dd
        for h in (0, 1):
            dB[i * 8:i * 8 + 8, h * HB:(h + 1) * HB] = s[h * 8:h * 8 + 8]

    factor = 2.0 * off_weight / SAMPLES

    def unstack(ref):
        g = ref[...].astype(F32)
        rows = ref.shape[0] * 8
        return [g[:, h * 8:h * 8 + 8, :].reshape(rows, HN).astype(BF16) for h in (0, 1)]

    def sum_messages(ref):
        t = ref[0]
        for i in range(1, ref.shape[0]):
            t = t + ref[i]
        return t

    wide_recv(5, gball)
    g0, g1 = unstack(gball)
    d = factor * (
        jnp.dot(g0, S_a[:HN, :], preferred_element_type=F32)
        + jnp.dot(g1, S_a[HN:, :], preferred_element_type=F32)
    ) + dA[...]
    narrow_recv(6, mar)
    total = sum_messages(mar)
    m1 = jnp.concatenate([total[q:q + 1, :Q] for q in range(4)], axis=1)
    m2 = jnp.concatenate([total[q + 4:q + 5, :Q] for q in range(4)], axis=1)
    inv = jnp.concatenate(inv_a, axis=1)
    grad = inv * (d - m1 - SR_a[...].astype(F32) * m2)
    for i in range(WN):
        ras[i] = jnp.concatenate(
            [grad[i * 8:i * 8 + 8, h * HS:(h + 1) * HS] for h in (0, 1)], axis=0).astype(BF16)
    wide_a2a(7, ras, rar)
    rar[w] = ras[w]
    lsend[...] = total[:, Q:]
    wide_bcast(8, lsend, lrecv)
    lrecv[w] = lsend[...]

    wide_recv(6, mbr)
    total = sum_messages(mbr)
    m1 = jnp.concatenate([total[q:q + 1] for q in range(4)], axis=1)
    m2 = jnp.concatenate([total[q + 4:q + 5] for q in range(4)], axis=1)
    inv = jnp.concatenate(inv_b, axis=1)
    own = pl.ds(pl.multiple_of(w * NN * 8, 16), NN * 8)
    rest = dB[...] - m1 - S_b[own, :].astype(F32) * m2
    narrow_recv(5, gaall)
    g0, g1 = unstack(gaall)
    d = factor * (
        jnp.dot(g0, S_b[:HN, :], preferred_element_type=F32)
        + jnp.dot(g1, S_b[HN:, :], preferred_element_type=F32)
    )
    grad = inv * (d + rest)
    for i in range(NN):
        rbs[i] = jnp.concatenate(
            [grad[i * 8:i * 8 + 8, h * HB:(h + 1) * HB] for h in (0, 1)], axis=0).astype(BF16)
    narrow_a2a(7, rbs, rbr)
    rbr[n] = rbs[n]

    wide_recv(7, rar)
    for i in range(WN):
        for h in (0, 1):
            ga_ref[:, i * SLAB + h * HS:i * SLAB + (h + 1) * HS] = rar[i, h * 8:h * 8 + 8, :]
    wide_recv(8, lrecv)
    loss_ref[...] = sum_messages(lrecv) / FEATS
    narrow_recv(7, rbr)
    for i in range(NN):
        for h in (0, 1):
            gb_ref[:, i * BLK + h * HB:i * BLK + (h + 1) * HB] = rbr[i, h * 8:h * 8 + 8, :]

    wide_sent(0, A3.at[n])
    narrow_sent(0, B3.at[w])
    wide_sent(1, B3)
    narrow_sent(1, A3)
    wide_sent(2, b1w)
    narrow_sent(2, a1n)
    wide_sent(3, gar)
    narrow_sent(3, gbr)
    diag_sent()
    wide_sent(5, gball)
    narrow_sent(5, gaall)
    wide_sent(6, mbr)
    narrow_sent(6, mar)
    wide_sent(7, rar)
    narrow_sent(7, rbr)
    wide_sent(8, lrecv)


def write_out(corr, loss, ga, gb, corr_out, loss_out, ga_out, gb_out, sem):
    rows = corr.shape[0] // 8
    copies = [
        pltpu.make_async_copy(
            corr.at[pl.ds(i * rows, rows)], corr_out.at[pl.ds(i * rows, rows)], sem.at[i])
        for i in range(8)
    ]
    copies.append(pltpu.make_async_copy(ga, ga_out, sem.at[8]))
    copies.append(pltpu.make_async_copy(gb, gb_out, sem.at[9]))
    for copy in copies:
        copy.start()
    loss_out[0, 0] = jnp.sum(loss[...])
    for copy in copies:
        copy.wait()


def solution(mesh):
    WN, NN = mesh.shape["wide"], mesh.shape["narrow"]

    def on_device(view_a, view_b):
        rows, features = view_a.shape
        samples = rows * WN * NN
        BLK = features // NN
        SLAB = features // WN
        HB, HS, HN = BLK // 2, SLAB // 2, samples // 2
        V = pltpu.VMEM
        vmem = pl.BlockSpec(memory_space=pltpu.VMEM)
        hbm = pl.BlockSpec(memory_space=pltpu.HBM)
        anywhere = pl.BlockSpec(memory_space=pl.ANY)
        dma = pltpu.SemaphoreType.DMA
        corr, loss, ga, gb = pl.pallas_call(
            functools.partial(kernel, WN, NN, BLK, samples),
            out_shape=(
                V((SLAB, BLK), BF16),
                V((8, 128), F32),
                V((rows, features), BF16),
                V((rows, features), BF16),
            ),
            in_specs=[hbm, hbm],
            out_specs=(vmem, vmem, vmem, vmem),
            scratch_shapes=[
                V((rows, features), BF16), V((rows, features), BF16), V((NN, 8, BLK), F32),
                V((WN, 16, HS), BF16), V((NN, 16, HB), BF16),
                V((WN, 16, HS), BF16), V((NN, 16, HB), BF16),
                V((NN, WN, 16, HS), BF16), V((WN, NN, 16, HB), BF16),
                V((WN, 16, HS), BF16), V((NN, 16, HB), BF16),
                V((samples, SLAB), BF16), V((samples, BLK), BF16), V((WN * 8, SLAB), BF16),
                V((WN, 16, HN), BF16), V((WN, 16, HN), BF16), V((NN, 16, HN), BF16),
                V((NN, 16, HN), BF16), V((NN, 16, HN), BF16), V((WN, 16, HN), BF16),
                V((8, BLK), F32), V((8, BLK), F32), V((8, BLK), F32), V((2, 8, BLK), F32),
                V((WN * 8, SLAB), F32), V((NN * 8, BLK), F32),
                V((8, SLAB // 4 + 128), F32), V((NN, 8, SLAB // 4 + 128), F32),
                V((8, BLK // 4), F32), V((WN, 8, BLK // 4), F32),
                V((2, 8, BLK), F32), V((8, BLK), F32),
                V((WN, 16, HS), BF16), V((WN, 16, HS), BF16),
                V((NN, 16, HB), BF16), V((NN, 16, HB), BF16),
                V((8, BLK), F32), V((8, 128), F32), V((WN, 8, 128), F32),
                dma((9,)), dma((9,)), dma((9,)), dma((9,)),
                dma((2, 20)), dma((7,)), dma((2,)), dma((2,)),
            ],
            compiler_params=pltpu.CompilerParams(
                collective_id=0, has_side_effects=True, vmem_limit_bytes=32 * 1024 * 1024),
        )(*(pltpu.with_memory_space_constraint(v, pltpu.HBM) for v in (view_a, view_b)))
        corr, loss, ga, gb = pl.pallas_call(
            write_out,
            out_shape=(
                jax.ShapeDtypeStruct((SLAB, BLK), BF16),
                jax.ShapeDtypeStruct((1, 1), F32),
                jax.ShapeDtypeStruct((rows, features), BF16),
                jax.ShapeDtypeStruct((rows, features), BF16),
            ),
            in_specs=[anywhere, vmem, anywhere, anywhere],
            out_specs=(anywhere, pl.BlockSpec(memory_space=pltpu.SMEM), anywhere, anywhere),
            scratch_shapes=[dma((10,))],
            compiler_params=pltpu.CompilerParams(vmem_limit_bytes=8 * 1024 * 1024),
        )(corr, loss, ga, gb)
        return corr, loss.reshape(()), ga, gb

    return jax.shard_map(
        on_device,
        mesh=mesh,
        in_specs=(P(("wide", "narrow"), None), P(("wide", "narrow"), None)),
        out_specs=(
            P("wide", "narrow"),
            P(),
            P(("wide", "narrow"), None),
            P(("wide", "narrow"), None),
        ),
        check_vma=False,
    )
```

```python
import functools

import jax
import jax.numpy as jnp
from jax import lax
from jax.experimental import pallas as pl
from jax.experimental.pallas import tpu as pltpu
from jax.sharding import PartitionSpec as P

off_weight = 0.0051
epsilon = 1e-05
MESH = pl.DeviceIdType.MESH
F32 = jnp.float32
BF16 = jnp.bfloat16


def kernel(
    WN, NN, BLK, SAMPLES,
    a_hbm, b_hbm,
    corr_ref, loss_ref, ga_ref, gb_ref,
    a_ref, b_ref, dummy,
    xa, xb, xb2, xa2,
    A3, B3, b1w, a1n,
    S_a, S_b, SR_a,
    gas, gar, gaall, gbs, gbr, gball,
    va, vb, Dn, Dw,
    dA, dB,
    mas, mar, mbs, mbr, ea, eb,
    ras, rar, rbs, rbr,
    lbuf, lsend, lrecv,
    s_w, r_w, s_n, r_n, r_a, r_b, r_d, in_sem,
):
    SLAB = BLK * (NN // WN)
    HB, HS = BLK // 2, SLAB // 2
    HN = SAMPLES // 2
    FEATS = BLK * NN
    w = lax.axis_index("wide")
    n = lax.axis_index("narrow")
    diag = lax.div(n, 2) == w

    z, y = lax.div(n, 4), lax.rem(n, 4)
    x, core = lax.div(w, 2), lax.rem(w, 2)

    def offset(j):
        return lax.rem(2 + 3 * j + 3 * lax.div(j * (j - 1), 2), 4)

    def wide_peer(i):
        return lax.rem(x + offset(lax.div(i, 2)), 4) * 2 + lax.rem(core + 1 - lax.rem(i, 2), 2)

    def narrow_peer(i):
        return lax.rem(z + offset(lax.div(i, 4)), 4) * 4 + lax.rem(y + offset(lax.rem(i, 4)), 4)

    def wide_copy(which, k, src, dst):
        return pltpu.make_async_remote_copy(
            src_ref=src, dst_ref=dst, send_sem=s_w.at[which], recv_sem=r_w.at[which],
            device_id=(wide_peer(k), n), device_id_type=MESH,
        )

    def narrow_copy(which, k, src, dst):
        return pltpu.make_async_remote_copy(
            src_ref=src, dst_ref=dst, send_sem=s_n.at[which], recv_sem=r_n.at[which],
            device_id=(w, narrow_peer(k)), device_id_type=MESH,
        )

    def each(count, body):
        def step(k, c):
            body(k)
            return c
        lax.fori_loop(0, count - 1, step, 0)


    def wide_recv(which, dst):
        ref = dst.at[pl.ds(0, WN - 1)]
        wide_copy(which, 1, ref, ref).wait_recv()

    def narrow_recv(which, dst):
        ref = dst.at[pl.ds(0, NN - 1)]
        narrow_copy(which, 1, ref, ref).wait_recv()

    def wide_sent(which, dst):
        ref = dst.at[pl.ds(0, WN - 1)]
        wide_copy(which, 1, ref, ref).wait_send()

    def narrow_sent(which, dst):
        ref = dst.at[pl.ds(0, NN - 1)]
        narrow_copy(which, 1, ref, ref).wait_send()

    def wide_a2a(which, src, dst):
        each(WN, lambda k: wide_copy(which, k, src.at[wide_peer(k)], dst.at[w]).start())

    def narrow_a2a(which, src, dst):
        each(NN, lambda k: narrow_copy(which, k, src.at[narrow_peer(k)], dst.at[n]).start())

    def wide_bcast(which, src, dst):
        each(WN, lambda k: wide_copy(which, k, src, dst.at[w]).start())

    def narrow_bcast(which, src, dst):
        each(NN, lambda k: narrow_copy(which, k, src, dst.at[n]).start())

    loads = [
        pltpu.make_async_copy(a_hbm, a_ref, in_sem.at[0]),
        pltpu.make_async_copy(b_hbm, b_ref, in_sem.at[1]),
    ]
    for load in loads:
        load.start()
    barrier = pltpu.get_barrier_semaphore()
    each(WN, lambda k: pl.semaphore_signal(
        barrier, inc=1, device_id=(wide_peer(k), n), device_id_type=MESH))
    each(NN, lambda k: pl.semaphore_signal(
        barrier, inc=1, device_id=(w, narrow_peer(k)), device_id_type=MESH))

    for load in loads:
        load.wait()

    def stack(ref, base, half):
        return jnp.concatenate(
            [ref[:, base:base + half], ref[:, base + half:base + 2 * half]], axis=0)

    for i in range(WN):
        xa[i] = stack(a_ref, i * SLAB, HS)
    for i in range(NN):
        xb[i] = stack(b_ref, i * BLK, HB)
    pl.semaphore_wait(barrier, WN + NN - 2)

    narrow_a2a(0, xb, B3.at[w])
    wide_a2a(0, xa, A3.at[n])
    A3[n, w] = xa[w]
    B3[w, n] = xb[n]
    for i in range(WN):
        xb2[i] = stack(b_ref, i * SLAB, HS)
    for i in range(NN):
        xa2[i] = stack(a_ref, i * BLK, HB)
    b1w[w] = xb2[w]
    a1n[n] = xa2[n]
    PART = WN // 2
    FULL, FIRST, SECOND = (0, PART), (0, PART // 2), (PART // 2, PART // 2)

    def slot(part, p, q):
        dz, dy = (q, p) if part == 0 else (p, q)
        return lax.rem(z + dz + 4, 4) * 4 + lax.rem(y + dy + 4, 4)

    def piece(part, at, cut):
        return A3.at[at, pl.ds(part * PART + cut[0], cut[1])]

    def move(part, index, at, cut, p, q):
        ref = piece(part, at, cut)
        return pltpu.make_async_remote_copy(
            src_ref=ref, dst_ref=ref, send_sem=s_n.at[1], recv_sem=r_a.at[part, index],
            device_id=(w, slot(part, p, q)), device_id_type=MESH,
        )

    LINES = (0, -1, 1, 2)

    def along(part, line, p, stage):
        step = (lambda d: (d, 0)) if stage == 1 else (lambda d: (0, d))
        for d, index in ((2, 3), (1, 0), (-1, 1)) if line == 3 else ((1, 0), (-1, 1)):
            move(part, line * 4 + index, slot(part, p, 0), FULL, *step(d)).start()

    def relay(part, line, p, stage):
        for d, index, cut in ((1, 2, FIRST), (-1, 3, SECOND)):
            got = slot(part, -d, 0) if stage == 1 else slot(part, p, -d)
            step = (d, 0) if stage == 1 else (0, d)
            move(part, line * 4 + index - 2, got, FULL, 0, 0).wait_recv()
            if line != 3:
                move(part, line * 4 + index, got, cut, *step).start()

    def far(part, line, p, stage):
        got = slot(part, 2, 0) if stage == 1 else slot(part, p, 2)
        for index, cut in ((3, FULL),) if line == 3 else ((2, FIRST), (3, SECOND)):
            move(part, line * 4 + index, got, cut, 0, 0).wait_recv()

    def move_b(index, at, dx, other):
        ref = B3.at[at]
        to = lax.rem(x + dx + 4, 4) * 2 + (1 - core if other else core)
        return pltpu.make_async_remote_copy(
            src_ref=ref, dst_ref=ref, send_sem=s_w.at[1], recv_sem=r_b.at[index],
            device_id=(to, n), device_id_type=MESH,
        )

    def slot_b(dx, other):
        return lax.rem(x + dx + 4, 4) * 2 + (1 - core if other else core)

    wide_recv(0, A3.at[n])
    for part in (0, 1):
        along(part, 4, 0, 1)
    for part in (0, 1):
        along(part, 0, 0, 2)
    narrow_recv(0, B3.at[w])
    for i, dx in enumerate((1, -1, 2)):
        move_b(i, w, dx, False).start()
    move_b(3, w, 0, True).start()
    def add_sums(ref, sums):
        def step(i, c):
            v = ref[i].astype(F32)
            return (c[0] + v, c[1] + v * v)
        return lax.fori_loop(0, ref.shape[0], step, sums, unroll=min(4, ref.shape[0]))

    def moments_of(sums):
        total, squares = sums

        def fold(t):
            return [jnp.sum(t[h * 8:(h + 1) * 8], axis=0, keepdims=True) / SAMPLES for h in (0, 1)]
        means, seconds = fold(total), fold(squares)
        invs = [lax.rsqrt(q - m * m + epsilon) for q, m in zip(seconds, means)]
        return means, invs

    def stacked(halves):
        return jnp.concatenate([jnp.broadcast_to(h, (8, h.shape[1])) for h in halves], axis=0)

    zero_b, zero_a = jnp.zeros((16, HB), F32), jnp.zeros((16, HS), F32)
    sums_b = add_sums(B3.at[w], (zero_b, zero_b))
    sums_a = add_sums(A3.at[n], (zero_a, zero_a))
    for part in (0, 1):
        relay(part, 4, 0, 1)
    for part in (0, 1):
        for line in (1, 2):
            along(part, line, LINES[line], 2)

    def take_b(i, dx, sums):
        got = slot_b(-dx, False)
        move_b(i, got, 0, False).wait_recv()
        move_b(4 + i, got, 0, True).start()
        return add_sums(B3.at[got], sums)

    def sums_of_piece(part, at, sums):
        return add_sums(piece(part, at, FULL), sums)

    for part in (0, 1):
        for p in (-1, 1):
            sums_a = sums_of_piece(part, slot(part, p, 0), sums_a)
    for part in (0, 1):
        relay(part, 0, 0, 2)
    for part in (0, 1):
        far(part, 4, 0, 1)
        along(part, 3, 2, 2)
    for i, dx in ((0, 1), (1, -1)):
        sums_b = take_b(i, dx, sums_b)
    for part in (0, 1):
        for line in (1, 2):
            relay(part, line, LINES[line], 2)
    sums_b = take_b(2, 2, sums_b)
    for i, dx in ((3, 0), (4, 1), (5, -1), (6, 2)):
        move_b(i, slot_b(-dx, True), 0, True).wait_recv()
        sums_b = add_sums(B3.at[slot_b(-dx, True)], sums_b)
    mean_b, inv_b = moments_of(sums_b)
    mean2, inv2 = stacked(mean_b), stacked(inv_b)

    def norm_b(i, c):
        src, pair = lax.div(i, NN // 2), lax.rem(i, NN // 2)
        even = (B3[src, 2 * pair].astype(F32) - mean2) * inv2
        odd = (B3[src, 2 * pair + 1].astype(F32) - mean2) * inv2
        at = pl.ds(pl.multiple_of(i * 16, 16), 16)
        for h in (0, 1):
            S_b[at, h * HB:(h + 1) * HB] = jnp.concatenate(
                [even[h * 8:h * 8 + 8], odd[h * 8:h * 8 + 8]], axis=0).astype(BF16)
        return c
    lax.fori_loop(0, SAMPLES // 16, norm_b, 0, unroll=2)

    dot_last = functools.partial(
        lax.dot_general, dimension_numbers=(((1,), (1,)), ((), ())), preferred_element_type=F32)

    def stack_gram(dst, g):
        count = g.shape[0] // 8
        g3 = g.reshape(count, 8, SAMPLES)
        dst[...] = jnp.concatenate([g3[:, :, :HN], g3[:, :, HN:]], axis=1).astype(BF16)

    own_rows = S_b[pl.ds(pl.multiple_of(w * NN * 8, 16), NN * 8), :]
    stack_gram(gbs, dot_last(own_rows, S_b[...]))
    narrow_a2a(3, gbs, gbr)
    gbr[n] = gbs[n]
    for part in (0, 1):
        relay(part, 3, 2, 2)
    wide_a2a(2, xb2, b1w)

    for part in (0, 1):
        for q in (-1, 1):
            sums_a = sums_of_piece(part, slot(part, 0, q), sums_a)
            for p in (-1, 1):
                sums_a = sums_of_piece(part, slot(part, p, q), sums_a)
        sums_a = sums_of_piece(part, slot(part, 2, 0), sums_a)
    for part in (0, 1):
        for q in (-1, 1):
            sums_a = sums_of_piece(part, slot(part, 2, q), sums_a)
    for line in range(4):
        for part in (0, 1):
            far(part, line, LINES[line], 2)
            sums_a = sums_of_piece(part, slot(part, LINES[line], 2), sums_a)
    mean_a, inv_a = moments_of(sums_a)
    mean2a, inv2a = stacked(mean_a), stacked(inv_a)

    def norm_a(i, c):
        src, pair = lax.div(i, NN // 2), lax.rem(i, NN // 2)
        even = (A3[2 * pair, src].astype(F32) - mean2a) * inv2a
        odd = (A3[2 * pair + 1, src].astype(F32) - mean2a) * inv2a
        at = pl.ds(pl.multiple_of(i * 16, 16), 16)
        for h in (0, 1):
            S_a[at, h * HS:(h + 1) * HS] = jnp.concatenate(
                [even[h * 8:h * 8 + 8], odd[h * 8:h * 8 + 8]], axis=0).astype(BF16)
        return c
    lax.fori_loop(0, SAMPLES // 16, norm_a, 0)
    for i in range(WN // 2):
        even = (A3[n, 2 * i].astype(F32) - mean2a) * inv2a
        odd = (A3[n, 2 * i + 1].astype(F32) - mean2a) * inv2a
        for h in (0, 1):
            SR_a[i * 16:i * 16 + 16, h * HS:(h + 1) * HS] = jnp.concatenate(
                [even[h * 8:h * 8 + 8], odd[h * 8:h * 8 + 8]], axis=0).astype(BF16)

    stack_gram(gas, dot_last(SR_a[...], S_a[...]))
    wide_a2a(3, gas, gar)
    gar[w] = gas[w]

    narrow_a2a(2, xa2, a1n)
    ones = jnp.ones((8, SAMPLES), BF16)
    mstd_a = jnp.dot(ones, S_a[...], preferred_element_type=F32) / SAMPLES
    mstd_b = jnp.dot(ones, S_b[...], preferred_element_type=F32) / SAMPLES

    half = lax.rem(n, 2)
    lbuf[...] = jnp.zeros_like(lbuf)
    ea[...] = jnp.zeros_like(ea)
    eb[...] = jnp.zeros_like(eb)

    def narrow_vec(k, h=None):
        h = half if h is None else h
        return pltpu.make_async_remote_copy(
            src_ref=vb, dst_ref=Dw.at[h], send_sem=s_n.at[4], recv_sem=r_d.at[h],
            device_id=(w, narrow_peer(k)), device_id_type=MESH,
        )

    @pl.when(diag)
    def _():
        def step(i, c):
            at = pl.ds(pl.multiple_of(i * 16, 16), 16)
            cols = pl.ds(pl.multiple_of(half * BLK, BLK), BLK)
            return c + S_a[at, cols].astype(F32) * S_b[at, :].astype(F32)
        prod = lax.fori_loop(0, SAMPLES // 16, step, jnp.zeros((16, BLK), F32), unroll=4)
        c = jnp.sum(prod, axis=0, keepdims=True) / SAMPLES
        d = -2.0 * (1.0 - c) - 2.0 * off_weight * c
        mb = jnp.concatenate(mean_b, axis=1)
        ib = jnp.concatenate(inv_b, axis=1)
        first = (half == 0).astype(F32)
        ma = mean_a[0] * first + mean_a[1] * (1.0 - first)
        ia = inv_a[0] * first + inv_a[1] * (1.0 - first)
        msa = mstd_a[0:1, :BLK] * first + mstd_a[0:1, BLK:] * (1.0 - first)
        pad = jnp.zeros((6, BLK), F32)
        ea[half] = jnp.concatenate([d * mstd_b[0:1], d * c, pad], axis=0)
        eb[...] = jnp.concatenate([d * msa, d * c, pad], axis=0)
        pad = jnp.zeros((5, BLK), F32)
        va[...] = jnp.concatenate([ma, ia, d, pad], axis=0)
        vb[...] = jnp.concatenate([mb, ib, d, pad], axis=0)
        Dn[...] = va[...]
        Dw[half] = vb[...]
        lbuf[0:1, :] = (1.0 - c) * (1.0 - c) - off_weight * c * c
        each(WN, lambda k: wide_copy(4, k, va, Dn).start())
        each(NN, lambda k: narrow_vec(k).start())

    def diag_recv():
        @pl.when(lax.div(n, 2) != w)
        def _():
            wide_copy(4, 1, va, Dn).wait_recv()
        for h in (0, 1):
            @pl.when(n != 2 * w + h)
            def _():
                narrow_vec(1, h).wait_recv()

    def diag_sent():
        @pl.when(diag)
        def _():
            ref = dummy.at[pl.ds(0, WN - 1)]
            wide_copy(4, 1, ref, ref).wait_send()
            ref = dummy.at[pl.ds(0, NN - 1)]
            narrow_copy(4, 1, ref, ref).wait_send()

    TM = SLAB // 2
    acc = jnp.zeros((8, BLK), F32)
    fb = jnp.zeros((8, BLK), F32)
    ones = jnp.ones((8, BLK), BF16)
    msb = mstd_b.astype(BF16)
    fa, sa = [], []
    for t in range(2):
        at = slice(t * TM, (t + 1) * TM)
        c = lax.dot_general(
            S_a[:, at], S_b[...], (((0,), (0,)), ((), ())), preferred_element_type=F32
        ) * (1.0 / SAMPLES)
        rounded = c.astype(BF16)
        corr_ref[at, :] = rounded
        squares = c * c
        acc = acc + jnp.sum(squares.reshape(TM // 8, 8, BLK), axis=0)
        fa.append(dot_last(msb, rounded)[0:1])
        sa.append(dot_last(ones, squares.astype(BF16))[0:1])
        fb = fb + jnp.dot(mstd_a[:, at].astype(BF16), rounded, preferred_element_type=F32)
    twice = 2.0 * off_weight
    m1 = jnp.concatenate([twice * fa[h] + ea[h, 0:1] for h in (0, 1)], axis=1)
    m2 = jnp.concatenate([twice * sa[h] + ea[h, 1:2] for h in (0, 1)], axis=1)
    Q = SLAB // 4
    lost = lbuf[...] + off_weight * acc
    mas[...] = jnp.concatenate(
        [jnp.concatenate([m[:, q * Q:(q + 1) * Q] for m in (m1, m2) for q in range(4)], axis=0)]
        + [sum(lost[:, q * 128:(q + 1) * 128] for q in range(BLK // 128))], axis=1)
    narrow_bcast(6, mas, mar)
    mar[n] = mas[...]
    m1 = twice * fb[0:1] + eb[0:1]
    m2 = twice * jnp.sum(acc, axis=0, keepdims=True) + eb[1:2]
    QB = BLK // 4
    mbs[...] = jnp.concatenate(
        [m[:, q * QB:(q + 1) * QB] for m in (m1, m2) for q in range(4)], axis=0)
    wide_bcast(6, mbs, mbr)
    mbr[w] = mbs[...]

    def total_of(ref):
        t = ref[0].astype(F32)
        for i in range(1, ref.shape[0]):
            t = t + ref[i].astype(F32)
        return t
    wide_recv(3, gar)
    gaall[n] = total_of(gar).astype(BF16)
    narrow_bcast(5, gaall.at[n], gaall)
    narrow_recv(3, gbr)
    gball[w] = total_of(gbr).astype(BF16)
    wide_bcast(5, gball.at[w], gball)

    wide_recv(2, b1w)
    narrow_recv(2, a1n)

    diag_recv()

    dmean, dinv, dd = (stacked([Dw[h, i:i + 1, :] for h in (0, 1)]) for i in range(3))
    for i in range(WN):
        s = ((b1w[i].astype(F32) - dmean) * dinv).astype(BF16).astype(F32) * dd
        for h in (0, 1):
            dA[i * 8:i * 8 + 8, h * HS:(h + 1) * HS] = s[h * 8:h * 8 + 8]
    dmean, dinv, dd = (
        stacked([Dn[i:i + 1, h * HB:(h + 1) * HB] for h in (0, 1)]) for i in range(3))
    for i in range(NN):
        s = ((a1n[i].astype(F32) - dmean) * dinv).astype(BF16).astype(F32) * dd
        for h in (0, 1):
            dB[i * 8:i * 8 + 8, h * HB:(h + 1) * HB] = s[h * 8:h * 8 + 8]

    factor = 2.0 * off_weight / SAMPLES

    def unstack(ref):
        g = ref[...].astype(F32)
        rows = ref.shape[0] * 8
        return [g[:, h * 8:h * 8 + 8, :].reshape(rows, HN).astype(BF16) for h in (0, 1)]

    def sum_messages(ref):
        t = ref[0]
        for i in range(1, ref.shape[0]):
            t = t + ref[i]
        return t

    wide_recv(5, gball)
    g0, g1 = unstack(gball)
    d = factor * (
        jnp.dot(g0, S_a[:HN, :], preferred_element_type=F32)
        + jnp.dot(g1, S_a[HN:, :], preferred_element_type=F32)
    ) + dA[...]
    narrow_recv(6, mar)
    total = sum_messages(mar)
    m1 = jnp.concatenate([total[q:q + 1, :Q] for q in range(4)], axis=1)
    m2 = jnp.concatenate([total[q + 4:q + 5, :Q] for q in range(4)], axis=1)
    inv = jnp.concatenate(inv_a, axis=1)
    grad = inv * (d - m1 - SR_a[...].astype(F32) * m2)
    for i in range(WN):
        ras[i] = jnp.concatenate(
            [grad[i * 8:i * 8 + 8, h * HS:(h + 1) * HS] for h in (0, 1)], axis=0).astype(BF16)
    wide_a2a(7, ras, rar)
    rar[w] = ras[w]
    lsend[...] = total[:, Q:]
    wide_bcast(8, lsend, lrecv)
    lrecv[w] = lsend[...]

    wide_recv(6, mbr)
    total = sum_messages(mbr)
    m1 = jnp.concatenate([total[q:q + 1] for q in range(4)], axis=1)
    m2 = jnp.concatenate([total[q + 4:q + 5] for q in range(4)], axis=1)
    inv = jnp.concatenate(inv_b, axis=1)
    own = pl.ds(pl.multiple_of(w * NN * 8, 16), NN * 8)
    rest = dB[...] - m1 - S_b[own, :].astype(F32) * m2
    narrow_recv(5, gaall)
    g0, g1 = unstack(gaall)
    d = factor * (
        jnp.dot(g0, S_b[:HN, :], preferred_element_type=F32)
        + jnp.dot(g1, S_b[HN:, :], preferred_element_type=F32)
    )
    grad = inv * (d + rest)
    for i in range(NN):
        rbs[i] = jnp.concatenate(
            [grad[i * 8:i * 8 + 8, h * HB:(h + 1) * HB] for h in (0, 1)], axis=0).astype(BF16)
    narrow_a2a(7, rbs, rbr)
    rbr[n] = rbs[n]

    wide_recv(7, rar)
    for i in range(WN):
        for h in (0, 1):
            ga_ref[:, i * SLAB + h * HS:i * SLAB + (h + 1) * HS] = rar[i, h * 8:h * 8 + 8, :]
    wide_recv(8, lrecv)
    loss = jnp.sum(sum_messages(lrecv), keepdims=True) / FEATS
    loss_ref[...] = jnp.broadcast_to(loss, loss_ref.shape)
    narrow_recv(7, rbr)
    for i in range(NN):
        for h in (0, 1):
            gb_ref[:, i * BLK + h * HB:i * BLK + (h + 1) * HB] = rbr[i, h * 8:h * 8 + 8, :]

    wide_sent(0, A3.at[n])
    narrow_sent(0, B3.at[w])
    wide_sent(1, B3)
    narrow_sent(1, A3)
    wide_sent(2, b1w)
    narrow_sent(2, a1n)
    wide_sent(3, gar)
    narrow_sent(3, gbr)
    diag_sent()
    wide_sent(5, gball)
    narrow_sent(5, gaall)
    wide_sent(6, mbr)
    narrow_sent(6, mar)
    wide_sent(7, rar)
    narrow_sent(7, rbr)
    wide_sent(8, lrecv)


def write_out(corr, loss, ga, gb, corr_out, loss_out, ga_out, gb_out, sem):
    rows = corr.shape[0] // 8
    copies = [
        pltpu.make_async_copy(
            corr.at[pl.ds(i * rows, rows)], corr_out.at[pl.ds(i * rows, rows)], sem.at[i])
        for i in range(8)
    ]
    copies.append(pltpu.make_async_copy(ga, ga_out, sem.at[8]))
    copies.append(pltpu.make_async_copy(gb, gb_out, sem.at[9]))
    copies.append(pltpu.make_async_copy(loss.at[pl.ds(0, 1)], loss_out, sem.at[10]))
    for copy in copies:
        copy.start()
    for copy in copies:
        copy.wait()


def solution(mesh):
    WN, NN = mesh.shape["wide"], mesh.shape["narrow"]

    def on_device(view_a, view_b):
        rows, features = view_a.shape
        samples = rows * WN * NN
        BLK = features // NN
        SLAB = features // WN
        HB, HS, HN = BLK // 2, SLAB // 2, samples // 2
        V = pltpu.VMEM
        vmem = pl.BlockSpec(memory_space=pltpu.VMEM)
        hbm = pl.BlockSpec(memory_space=pltpu.HBM)
        anywhere = pl.BlockSpec(memory_space=pl.ANY)
        dma = pltpu.SemaphoreType.DMA
        corr, loss, ga, gb = pl.pallas_call(
            functools.partial(kernel, WN, NN, BLK, samples),
            out_shape=(
                V((SLAB, BLK), BF16),
                V((8, 128), F32),
                V((rows, features), BF16),
                V((rows, features), BF16),
            ),
            in_specs=[hbm, hbm],
            out_specs=(vmem, vmem, vmem, vmem),
            scratch_shapes=[
                V((rows, features), BF16), V((rows, features), BF16), V((NN, 8, BLK), F32),
                V((WN, 16, HS), BF16), V((NN, 16, HB), BF16),
                V((WN, 16, HS), BF16), V((NN, 16, HB), BF16),
                V((NN, WN, 16, HS), BF16), V((WN, NN, 16, HB), BF16),
                V((WN, 16, HS), BF16), V((NN, 16, HB), BF16),
                V((samples, SLAB), BF16), V((samples, BLK), BF16), V((WN * 8, SLAB), BF16),
                V((WN, 16, HN), BF16), V((WN, 16, HN), BF16), V((NN, 16, HN), BF16),
                V((NN, 16, HN), BF16), V((NN, 16, HN), BF16), V((WN, 16, HN), BF16),
                V((8, BLK), F32), V((8, BLK), F32), V((8, BLK), F32), V((2, 8, BLK), F32),
                V((WN * 8, SLAB), F32), V((NN * 8, BLK), F32),
                V((8, SLAB // 4 + 128), F32), V((NN, 8, SLAB // 4 + 128), F32),
                V((8, BLK // 4), F32), V((WN, 8, BLK // 4), F32),
                V((2, 8, BLK), F32), V((8, BLK), F32),
                V((WN, 16, HS), BF16), V((WN, 16, HS), BF16),
                V((NN, 16, HB), BF16), V((NN, 16, HB), BF16),
                V((8, BLK), F32), V((8, 128), F32), V((WN, 8, 128), F32),
                dma((9,)), dma((9,)), dma((9,)), dma((9,)),
                dma((2, 20)), dma((7,)), dma((2,)), dma((2,)),
            ],
            compiler_params=pltpu.CompilerParams(
                collective_id=0, has_side_effects=True, vmem_limit_bytes=32 * 1024 * 1024),
        )(*(pltpu.with_memory_space_constraint(v, pltpu.HBM) for v in (view_a, view_b)))
        corr, loss, ga, gb = pl.pallas_call(
            write_out,
            out_shape=(
                jax.ShapeDtypeStruct((SLAB, BLK), BF16),
                jax.ShapeDtypeStruct((1, 128), F32),
                jax.ShapeDtypeStruct((rows, features), BF16),
                jax.ShapeDtypeStruct((rows, features), BF16),
            ),
            in_specs=[anywhere] * 4,
            out_specs=(anywhere,) * 4,
            scratch_shapes=[dma((11,))],
            compiler_params=pltpu.CompilerParams(vmem_limit_bytes=8 * 1024 * 1024),
        )(corr, loss, ga, gb)
        return corr, loss[0, 0], ga, gb

    return jax.shard_map(
        on_device,
        mesh=mesh,
        in_specs=(P(("wide", "narrow"), None), P(("wide", "narrow"), None)),
        out_specs=(
            P("wide", "narrow"),
            P(),
            P(("wide", "narrow"), None),
            P(("wide", "narrow"), None),
        ),
        check_vma=False,
    )
```

```python
import functools

import jax
import jax.numpy as jnp
from jax import lax
from jax.experimental import pallas as pl
from jax.experimental.pallas import tpu as pltpu
from jax.sharding import PartitionSpec as P

off_weight = 0.0051
epsilon = 1e-05
MESH = pl.DeviceIdType.MESH
F32 = jnp.float32
BF16 = jnp.bfloat16


def kernel(
    WN, NN, BLK, SAMPLES,
    a_hbm, b_hbm,
    corr_ref, loss_ref, ga_ref, gb_ref,
    a_ref, b_ref, dummy,
    xa, xb, xb2, xa2,
    A3, B3, b1w, a1n,
    S_a, S_b, SR_a,
    gas, gar, gaall, gbs, gbr, gball,
    va, vb, Dn, Dw,
    dA, dB,
    mas, mar, mbs, mbr, ea, eb,
    ras, rar, rbs, rbr,
    lbuf, lsend, lrecv,
    s_w, r_w, s_n, r_n, r_a, r_b, r_d, in_sem,
):
    SLAB = BLK * (NN // WN)
    HB, HS = BLK // 2, SLAB // 2
    HN = SAMPLES // 2
    FEATS = BLK * NN
    w = lax.axis_index("wide")
    n = lax.axis_index("narrow")
    diag = lax.div(n, 2) == w

    z, y = lax.div(n, 4), lax.rem(n, 4)
    x, core = lax.div(w, 2), lax.rem(w, 2)

    def offset(j):
        return lax.rem(2 + 3 * j + 3 * lax.div(j * (j - 1), 2), 4)

    def wide_peer(i):
        return lax.rem(x + offset(lax.div(i, 2)), 4) * 2 + lax.rem(core + 1 - lax.rem(i, 2), 2)

    def narrow_peer(i):
        return lax.rem(z + offset(lax.div(i, 4)), 4) * 4 + lax.rem(y + offset(lax.rem(i, 4)), 4)

    def wide_copy(which, k, src, dst):
        return pltpu.make_async_remote_copy(
            src_ref=src, dst_ref=dst, send_sem=s_w.at[which], recv_sem=r_w.at[which],
            device_id=(wide_peer(k), n), device_id_type=MESH,
        )

    def narrow_copy(which, k, src, dst):
        return pltpu.make_async_remote_copy(
            src_ref=src, dst_ref=dst, send_sem=s_n.at[which], recv_sem=r_n.at[which],
            device_id=(w, narrow_peer(k)), device_id_type=MESH,
        )

    def each(count, body):
        def step(k, c):
            body(k)
            return c
        lax.fori_loop(0, count - 1, step, 0)


    def wide_recv(which, dst):
        ref = dst.at[pl.ds(0, WN - 1)]
        wide_copy(which, 1, ref, ref).wait_recv()

    def narrow_recv(which, dst):
        ref = dst.at[pl.ds(0, NN - 1)]
        narrow_copy(which, 1, ref, ref).wait_recv()

    def wide_sent(which, dst):
        ref = dst.at[pl.ds(0, WN - 1)]
        wide_copy(which, 1, ref, ref).wait_send()

    def narrow_sent(which, dst):
        ref = dst.at[pl.ds(0, NN - 1)]
        narrow_copy(which, 1, ref, ref).wait_send()

    def wide_a2a(which, src, dst):
        each(WN, lambda k: wide_copy(which, k, src.at[wide_peer(k)], dst.at[w]).start())

    def narrow_a2a(which, src, dst):
        each(NN, lambda k: narrow_copy(which, k, src.at[narrow_peer(k)], dst.at[n]).start())

    def wide_bcast(which, src, dst):
        each(WN, lambda k: wide_copy(which, k, src, dst.at[w]).start())

    def narrow_bcast(which, src, dst):
        each(NN, lambda k: narrow_copy(which, k, src, dst.at[n]).start())

    loads = [
        pltpu.make_async_copy(a_hbm, a_ref, in_sem.at[0]),
        pltpu.make_async_copy(b_hbm, b_ref, in_sem.at[1]),
    ]
    for load in loads:
        load.start()
    barrier = pltpu.get_barrier_semaphore()
    each(WN, lambda k: pl.semaphore_signal(
        barrier, inc=1, device_id=(wide_peer(k), n), device_id_type=MESH))
    each(NN, lambda k: pl.semaphore_signal(
        barrier, inc=1, device_id=(w, narrow_peer(k)), device_id_type=MESH))

    for load in loads:
        load.wait()

    def stack(ref, base, half):
        return jnp.concatenate(
            [ref[:, base:base + half], ref[:, base + half:base + 2 * half]], axis=0)

    for i in range(WN):
        xa[i] = stack(a_ref, i * SLAB, HS)
    for i in range(NN):
        xb[i] = stack(b_ref, i * BLK, HB)
    pl.semaphore_wait(barrier, WN + NN - 2)

    narrow_a2a(0, xb, B3.at[w])
    wide_a2a(0, xa, A3.at[n])
    A3[n, w] = xa[w]
    B3[w, n] = xb[n]
    for i in range(WN):
        xb2[i] = stack(b_ref, i * SLAB, HS)
    for i in range(NN):
        xa2[i] = stack(a_ref, i * BLK, HB)
    b1w[w] = xb2[w]
    a1n[n] = xa2[n]
    PART = WN // 2
    FULL, FIRST, SECOND = (0, PART), (0, PART // 2), (PART // 2, PART // 2)

    def slot(part, p, q):
        dz, dy = (q, p) if part == 0 else (p, q)
        return lax.rem(z + dz + 4, 4) * 4 + lax.rem(y + dy + 4, 4)

    def piece(part, at, cut):
        return A3.at[at, pl.ds(part * PART + cut[0], cut[1])]

    def move(part, index, at, cut, p, q):
        ref = piece(part, at, cut)
        return pltpu.make_async_remote_copy(
            src_ref=ref, dst_ref=ref, send_sem=s_n.at[1], recv_sem=r_a.at[part, index],
            device_id=(w, slot(part, p, q)), device_id_type=MESH,
        )

    LINES = (0, -1, 1, 2)

    def along(part, line, p, stage):
        step = (lambda d: (d, 0)) if stage == 1 else (lambda d: (0, d))
        for d, index in ((2, 3), (1, 0), (-1, 1)) if line == 3 else ((1, 0), (-1, 1)):
            move(part, line * 4 + index, slot(part, p, 0), FULL, *step(d)).start()

    def relay(part, line, p, stage):
        for d, index, cut in ((1, 2, FIRST), (-1, 3, SECOND)):
            got = slot(part, -d, 0) if stage == 1 else slot(part, p, -d)
            step = (d, 0) if stage == 1 else (0, d)
            move(part, line * 4 + index - 2, got, FULL, 0, 0).wait_recv()
            if line != 3:
                move(part, line * 4 + index, got, cut, *step).start()

    def far(part, line, p, stage):
        got = slot(part, 2, 0) if stage == 1 else slot(part, p, 2)
        for index, cut in ((3, FULL),) if line == 3 else ((2, FIRST), (3, SECOND)):
            move(part, line * 4 + index, got, cut, 0, 0).wait_recv()

    def move_b(index, at, dx, other):
        ref = B3.at[at]
        to = lax.rem(x + dx + 4, 4) * 2 + (1 - core if other else core)
        return pltpu.make_async_remote_copy(
            src_ref=ref, dst_ref=ref, send_sem=s_w.at[1], recv_sem=r_b.at[index],
            device_id=(to, n), device_id_type=MESH,
        )

    def slot_b(dx, other):
        return lax.rem(x + dx + 4, 4) * 2 + (1 - core if other else core)

    wide_recv(0, A3.at[n])
    for part in (0, 1):
        along(part, 4, 0, 1)
    for part in (0, 1):
        along(part, 0, 0, 2)
    narrow_recv(0, B3.at[w])
    for i, dx in enumerate((1, -1, 2)):
        move_b(i, w, dx, False).start()
    move_b(3, w, 0, True).start()
    def add_sums(ref, sums):
        def step(i, c):
            v = ref[i].astype(F32)
            return (c[0] + v, c[1] + v * v)
        return lax.fori_loop(0, ref.shape[0], step, sums, unroll=min(4, ref.shape[0]))

    def moments_of(sums):
        total, squares = sums

        def fold(t):
            return [jnp.sum(t[h * 8:(h + 1) * 8], axis=0, keepdims=True) / SAMPLES for h in (0, 1)]
        means, seconds = fold(total), fold(squares)
        invs = [lax.rsqrt(q - m * m + epsilon) for q, m in zip(seconds, means)]
        return means, invs

    def stacked(halves):
        return jnp.concatenate([jnp.broadcast_to(h, (8, h.shape[1])) for h in halves], axis=0)

    zero_b, zero_a = jnp.zeros((16, HB), F32), jnp.zeros((16, HS), F32)
    sums_b = add_sums(B3.at[w], (zero_b, zero_b))
    sums_a = add_sums(A3.at[n], (zero_a, zero_a))
    for part in (0, 1):
        relay(part, 4, 0, 1)
    for part in (0, 1):
        for line in (1, 2):
            along(part, line, LINES[line], 2)

    def take_b(i, dx, sums):
        got = slot_b(-dx, False)
        move_b(i, got, 0, False).wait_recv()
        move_b(4 + i, got, 0, True).start()
        return add_sums(B3.at[got], sums)

    def sums_of_piece(part, at, sums):
        return add_sums(piece(part, at, FULL), sums)

    for part in (0, 1):
        for p in (-1, 1):
            sums_a = sums_of_piece(part, slot(part, p, 0), sums_a)
    for part in (0, 1):
        relay(part, 0, 0, 2)
    for part in (0, 1):
        far(part, 4, 0, 1)
        along(part, 3, 2, 2)
    for i, dx in ((0, 1), (1, -1)):
        sums_b = take_b(i, dx, sums_b)
    for part in (0, 1):
        for line in (1, 2):
            relay(part, line, LINES[line], 2)
    sums_b = take_b(2, 2, sums_b)
    for i, dx in ((3, 0), (4, 1), (5, -1), (6, 2)):
        move_b(i, slot_b(-dx, True), 0, True).wait_recv()
        sums_b = add_sums(B3.at[slot_b(-dx, True)], sums_b)
    mean_b, inv_b = moments_of(sums_b)
    mean2, inv2 = stacked(mean_b), stacked(inv_b)

    def norm_b(i, c):
        src, pair = lax.div(i, NN // 2), lax.rem(i, NN // 2)
        even = (B3[src, 2 * pair].astype(F32) - mean2) * inv2
        odd = (B3[src, 2 * pair + 1].astype(F32) - mean2) * inv2
        at = pl.ds(pl.multiple_of(i * 16, 16), 16)
        for h in (0, 1):
            S_b[at, h * HB:(h + 1) * HB] = jnp.concatenate(
                [even[h * 8:h * 8 + 8], odd[h * 8:h * 8 + 8]], axis=0).astype(BF16)
        return c
    lax.fori_loop(0, SAMPLES // 16, norm_b, 0, unroll=2)

    dot_last = functools.partial(
        lax.dot_general, dimension_numbers=(((1,), (1,)), ((), ())), preferred_element_type=F32)

    def stack_gram(dst, g):
        count = g.shape[0] // 8
        g3 = g.reshape(count, 8, SAMPLES)
        dst[...] = jnp.concatenate([g3[:, :, :HN], g3[:, :, HN:]], axis=1).astype(BF16)

    own_rows = S_b[pl.ds(pl.multiple_of(w * NN * 8, 16), NN * 8), :]
    stack_gram(gbs, dot_last(own_rows, S_b[...]))
    narrow_a2a(3, gbs, gbr)
    gbr[n] = gbs[n]
    for part in (0, 1):
        relay(part, 3, 2, 2)
    wide_a2a(2, xb2, b1w)
    narrow_a2a(2, xa2, a1n)

    for part in (0, 1):
        for q in (-1, 1):
            sums_a = sums_of_piece(part, slot(part, 0, q), sums_a)
            for p in (-1, 1):
                sums_a = sums_of_piece(part, slot(part, p, q), sums_a)
        sums_a = sums_of_piece(part, slot(part, 2, 0), sums_a)
    for part in (0, 1):
        for q in (-1, 1):
            sums_a = sums_of_piece(part, slot(part, 2, q), sums_a)
    for line in range(4):
        for part in (0, 1):
            far(part, line, LINES[line], 2)
            sums_a = sums_of_piece(part, slot(part, LINES[line], 2), sums_a)
    mean_a, inv_a = moments_of(sums_a)
    mean2a, inv2a = stacked(mean_a), stacked(inv_a)

    def norm_a(i, c):
        src, pair = lax.div(i, NN // 2), lax.rem(i, NN // 2)
        even = (A3[2 * pair, src].astype(F32) - mean2a) * inv2a
        odd = (A3[2 * pair + 1, src].astype(F32) - mean2a) * inv2a
        at = pl.ds(pl.multiple_of(i * 16, 16), 16)
        for h in (0, 1):
            S_a[at, h * HS:(h + 1) * HS] = jnp.concatenate(
                [even[h * 8:h * 8 + 8], odd[h * 8:h * 8 + 8]], axis=0).astype(BF16)
        return c
    lax.fori_loop(0, SAMPLES // 16, norm_a, 0)
    for i in range(WN // 2):
        even = (A3[n, 2 * i].astype(F32) - mean2a) * inv2a
        odd = (A3[n, 2 * i + 1].astype(F32) - mean2a) * inv2a
        for h in (0, 1):
            SR_a[i * 16:i * 16 + 16, h * HS:(h + 1) * HS] = jnp.concatenate(
                [even[h * 8:h * 8 + 8], odd[h * 8:h * 8 + 8]], axis=0).astype(BF16)

    stack_gram(gas, dot_last(SR_a[...], S_a[...]))
    wide_a2a(3, gas, gar)
    gar[w] = gas[w]

    ones = jnp.ones((8, SAMPLES), BF16)
    mstd_a = jnp.dot(ones, S_a[...], preferred_element_type=F32) / SAMPLES
    mstd_b = jnp.dot(ones, S_b[...], preferred_element_type=F32) / SAMPLES

    half = lax.rem(n, 2)
    lbuf[...] = jnp.zeros_like(lbuf)
    ea[...] = jnp.zeros_like(ea)
    eb[...] = jnp.zeros_like(eb)

    def narrow_vec(k, h=None):
        h = half if h is None else h
        return pltpu.make_async_remote_copy(
            src_ref=vb, dst_ref=Dw.at[h], send_sem=s_n.at[4], recv_sem=r_d.at[h],
            device_id=(w, narrow_peer(k)), device_id_type=MESH,
        )

    @pl.when(diag)
    def _():
        def step(i, c):
            at = pl.ds(pl.multiple_of(i * 16, 16), 16)
            cols = pl.ds(pl.multiple_of(half * BLK, BLK), BLK)
            return c + S_a[at, cols].astype(F32) * S_b[at, :].astype(F32)
        prod = lax.fori_loop(0, SAMPLES // 16, step, jnp.zeros((16, BLK), F32), unroll=4)
        c = jnp.sum(prod, axis=0, keepdims=True) / SAMPLES
        d = -2.0 * (1.0 - c) - 2.0 * off_weight * c
        mb = jnp.concatenate(mean_b, axis=1)
        ib = jnp.concatenate(inv_b, axis=1)
        first = (half == 0).astype(F32)
        ma = mean_a[0] * first + mean_a[1] * (1.0 - first)
        ia = inv_a[0] * first + inv_a[1] * (1.0 - first)
        msa = mstd_a[0:1, :BLK] * first + mstd_a[0:1, BLK:] * (1.0 - first)
        pad = jnp.zeros((6, BLK), F32)
        ea[half] = jnp.concatenate([d * mstd_b[0:1], d * c, pad], axis=0)
        eb[...] = jnp.concatenate([d * msa, d * c, pad], axis=0)
        pad = jnp.zeros((5, BLK), F32)
        va[...] = jnp.concatenate([ma, ia, d, pad], axis=0)
        vb[...] = jnp.concatenate([mb, ib, d, pad], axis=0)
        Dn[...] = va[...]
        Dw[half] = vb[...]
        lbuf[0:1, :] = (1.0 - c) * (1.0 - c) - off_weight * c * c
        each(WN, lambda k: wide_copy(4, k, va, Dn).start())
        each(NN, lambda k: narrow_vec(k).start())

    def diag_recv():
        @pl.when(lax.div(n, 2) != w)
        def _():
            wide_copy(4, 1, va, Dn).wait_recv()
        for h in (0, 1):
            @pl.when(n != 2 * w + h)
            def _():
                narrow_vec(1, h).wait_recv()

    def diag_sent():
        @pl.when(diag)
        def _():
            ref = dummy.at[pl.ds(0, WN - 1)]
            wide_copy(4, 1, ref, ref).wait_send()
            ref = dummy.at[pl.ds(0, NN - 1)]
            narrow_copy(4, 1, ref, ref).wait_send()

    TM = SLAB // 2
    acc = jnp.zeros((8, BLK), F32)
    fb = jnp.zeros((8, BLK), F32)
    ones = jnp.ones((8, BLK), BF16)
    msb = mstd_b.astype(BF16)
    fa, sa = [], []
    for t in range(2):
        at = slice(t * TM, (t + 1) * TM)
        c = lax.dot_general(
            S_a[:, at], S_b[...], (((0,), (0,)), ((), ())), preferred_element_type=F32
        ) * (1.0 / SAMPLES)
        rounded = c.astype(BF16)
        corr_ref[at, :] = rounded
        squares = c * c
        acc = acc + jnp.sum(squares.reshape(TM // 8, 8, BLK), axis=0)
        fa.append(dot_last(msb, rounded)[0:1])
        sa.append(dot_last(ones, squares.astype(BF16))[0:1])
        fb = fb + jnp.dot(mstd_a[:, at].astype(BF16), rounded, preferred_element_type=F32)
    twice = 2.0 * off_weight
    m1 = jnp.concatenate([twice * fa[h] + ea[h, 0:1] for h in (0, 1)], axis=1)
    m2 = jnp.concatenate([twice * sa[h] + ea[h, 1:2] for h in (0, 1)], axis=1)
    Q = SLAB // 4
    lost = lbuf[...] + off_weight * acc
    mas[...] = jnp.concatenate(
        [jnp.concatenate([m[:, q * Q:(q + 1) * Q] for m in (m1, m2) for q in range(4)], axis=0)]
        + [sum(lost[:, q * 128:(q + 1) * 128] for q in range(BLK // 128))], axis=1)
    narrow_bcast(6, mas, mar)
    mar[n] = mas[...]
    m1 = twice * fb[0:1] + eb[0:1]
    m2 = twice * jnp.sum(acc, axis=0, keepdims=True) + eb[1:2]
    QB = BLK // 4
    mbs[...] = jnp.concatenate(
        [m[:, q * QB:(q + 1) * QB] for m in (m1, m2) for q in range(4)], axis=0)
    wide_bcast(6, mbs, mbr)
    mbr[w] = mbs[...]

    def total_of(ref):
        t = ref[0].astype(F32)
        for i in range(1, ref.shape[0]):
            t = t + ref[i].astype(F32)
        return t
    narrow_recv(3, gbr)
    gball[w] = total_of(gbr).astype(BF16)
    wide_bcast(5, gball.at[w], gball)
    wide_recv(3, gar)
    gaall[n] = total_of(gar).astype(BF16)
    narrow_bcast(5, gaall.at[n], gaall)

    wide_recv(2, b1w)
    narrow_recv(2, a1n)

    diag_recv()

    dmean, dinv, dd = (stacked([Dw[h, i:i + 1, :] for h in (0, 1)]) for i in range(3))
    for i in range(WN):
        s = ((b1w[i].astype(F32) - dmean) * dinv).astype(BF16).astype(F32) * dd
        for h in (0, 1):
            dA[i * 8:i * 8 + 8, h * HS:(h + 1) * HS] = s[h * 8:h * 8 + 8]
    dmean, dinv, dd = (
        stacked([Dn[i:i + 1, h * HB:(h + 1) * HB] for h in (0, 1)]) for i in range(3))
    for i in range(NN):
        s = ((a1n[i].astype(F32) - dmean) * dinv).astype(BF16).astype(F32) * dd
        for h in (0, 1):
            dB[i * 8:i * 8 + 8, h * HB:(h + 1) * HB] = s[h * 8:h * 8 + 8]

    factor = 2.0 * off_weight / SAMPLES

    def unstack(ref):
        g = ref[...].astype(F32)
        rows = ref.shape[0] * 8
        return [g[:, h * 8:h * 8 + 8, :].reshape(rows, HN).astype(BF16) for h in (0, 1)]

    def sum_messages(ref):
        t = ref[0]
        for i in range(1, ref.shape[0]):
            t = t + ref[i]
        return t

    wide_recv(5, gball)
    g0, g1 = unstack(gball)
    d = factor * (
        jnp.dot(g0, S_a[:HN, :], preferred_element_type=F32)
        + jnp.dot(g1, S_a[HN:, :], preferred_element_type=F32)
    ) + dA[...]
    narrow_recv(6, mar)
    total = sum_messages(mar)
    m1 = jnp.concatenate([total[q:q + 1, :Q] for q in range(4)], axis=1)
    m2 = jnp.concatenate([total[q + 4:q + 5, :Q] for q in range(4)], axis=1)
    inv = jnp.concatenate(inv_a, axis=1)
    grad = inv * (d - m1 - SR_a[...].astype(F32) * m2)
    for i in range(WN):
        ras[i] = jnp.concatenate(
            [grad[i * 8:i * 8 + 8, h * HS:(h + 1) * HS] for h in (0, 1)], axis=0).astype(BF16)
    wide_a2a(7, ras, rar)
    rar[w] = ras[w]
    lsend[...] = total[:, Q:]
    wide_bcast(8, lsend, lrecv)
    lrecv[w] = lsend[...]

    wide_recv(6, mbr)
    total = sum_messages(mbr)
    m1 = jnp.concatenate([total[q:q + 1] for q in range(4)], axis=1)
    m2 = jnp.concatenate([total[q + 4:q + 5] for q in range(4)], axis=1)
    inv = jnp.concatenate(inv_b, axis=1)
    own = pl.ds(pl.multiple_of(w * NN * 8, 16), NN * 8)
    rest = dB[...] - m1 - S_b[own, :].astype(F32) * m2
    narrow_recv(5, gaall)
    g0, g1 = unstack(gaall)
    d = factor * (
        jnp.dot(g0, S_b[:HN, :], preferred_element_type=F32)
        + jnp.dot(g1, S_b[HN:, :], preferred_element_type=F32)
    )
    grad = inv * (d + rest)
    for i in range(NN):
        rbs[i] = jnp.concatenate(
            [grad[i * 8:i * 8 + 8, h * HB:(h + 1) * HB] for h in (0, 1)], axis=0).astype(BF16)
    narrow_a2a(7, rbs, rbr)
    rbr[n] = rbs[n]

    wide_recv(7, rar)
    for i in range(WN):
        for h in (0, 1):
            ga_ref[:, i * SLAB + h * HS:i * SLAB + (h + 1) * HS] = rar[i, h * 8:h * 8 + 8, :]
    wide_recv(8, lrecv)
    loss = jnp.sum(sum_messages(lrecv), keepdims=True) / FEATS
    loss_ref[...] = jnp.broadcast_to(loss, loss_ref.shape)
    narrow_recv(7, rbr)
    for i in range(NN):
        for h in (0, 1):
            gb_ref[:, i * BLK + h * HB:i * BLK + (h + 1) * HB] = rbr[i, h * 8:h * 8 + 8, :]

    wide_sent(0, A3.at[n])
    narrow_sent(0, B3.at[w])
    wide_sent(1, B3)
    narrow_sent(1, A3)
    wide_sent(2, b1w)
    narrow_sent(2, a1n)
    wide_sent(3, gar)
    narrow_sent(3, gbr)
    diag_sent()
    wide_sent(5, gball)
    narrow_sent(5, gaall)
    wide_sent(6, mbr)
    narrow_sent(6, mar)
    wide_sent(7, rar)
    narrow_sent(7, rbr)
    wide_sent(8, lrecv)


def write_out(corr, loss, ga, gb, corr_out, loss_out, ga_out, gb_out, sem):
    rows = corr.shape[0] // 8
    copies = [
        pltpu.make_async_copy(
            corr.at[pl.ds(i * rows, rows)], corr_out.at[pl.ds(i * rows, rows)], sem.at[i])
        for i in range(8)
    ]
    copies.append(pltpu.make_async_copy(ga, ga_out, sem.at[8]))
    copies.append(pltpu.make_async_copy(gb, gb_out, sem.at[9]))
    copies.append(pltpu.make_async_copy(loss.at[pl.ds(0, 1)], loss_out, sem.at[10]))
    for copy in copies:
        copy.start()
    for copy in copies:
        copy.wait()


def solution(mesh):
    WN, NN = mesh.shape["wide"], mesh.shape["narrow"]

    def on_device(view_a, view_b):
        rows, features = view_a.shape
        samples = rows * WN * NN
        BLK = features // NN
        SLAB = features // WN
        HB, HS, HN = BLK // 2, SLAB // 2, samples // 2
        V = pltpu.VMEM
        vmem = pl.BlockSpec(memory_space=pltpu.VMEM)
        hbm = pl.BlockSpec(memory_space=pltpu.HBM)
        anywhere = pl.BlockSpec(memory_space=pl.ANY)
        dma = pltpu.SemaphoreType.DMA
        corr, loss, ga, gb = pl.pallas_call(
            functools.partial(kernel, WN, NN, BLK, samples),
            out_shape=(
                V((SLAB, BLK), BF16),
                V((8, 128), F32),
                V((rows, features), BF16),
                V((rows, features), BF16),
            ),
            in_specs=[hbm, hbm],
            out_specs=(vmem, vmem, vmem, vmem),
            scratch_shapes=[
                V((rows, features), BF16), V((rows, features), BF16), V((NN, 8, BLK), F32),
                V((WN, 16, HS), BF16), V((NN, 16, HB), BF16),
                V((WN, 16, HS), BF16), V((NN, 16, HB), BF16),
                V((NN, WN, 16, HS), BF16), V((WN, NN, 16, HB), BF16),
                V((WN, 16, HS), BF16), V((NN, 16, HB), BF16),
                V((samples, SLAB), BF16), V((samples, BLK), BF16), V((WN * 8, SLAB), BF16),
                V((WN, 16, HN), BF16), V((WN, 16, HN), BF16), V((NN, 16, HN), BF16),
                V((NN, 16, HN), BF16), V((NN, 16, HN), BF16), V((WN, 16, HN), BF16),
                V((8, BLK), F32), V((8, BLK), F32), V((8, BLK), F32), V((2, 8, BLK), F32),
                V((WN * 8, SLAB), F32), V((NN * 8, BLK), F32),
                V((8, SLAB // 4 + 128), F32), V((NN, 8, SLAB // 4 + 128), F32),
                V((8, BLK // 4), F32), V((WN, 8, BLK // 4), F32),
                V((2, 8, BLK), F32), V((8, BLK), F32),
                V((WN, 16, HS), BF16), V((WN, 16, HS), BF16),
                V((NN, 16, HB), BF16), V((NN, 16, HB), BF16),
                V((8, BLK), F32), V((8, 128), F32), V((WN, 8, 128), F32),
                dma((9,)), dma((9,)), dma((9,)), dma((9,)),
                dma((2, 20)), dma((7,)), dma((2,)), dma((2,)),
            ],
            compiler_params=pltpu.CompilerParams(
                collective_id=0, has_side_effects=True, vmem_limit_bytes=32 * 1024 * 1024),
        )(*(pltpu.with_memory_space_constraint(v, pltpu.HBM) for v in (view_a, view_b)))
        corr, loss, ga, gb = pl.pallas_call(
            write_out,
            out_shape=(
                jax.ShapeDtypeStruct((SLAB, BLK), BF16),
                jax.ShapeDtypeStruct((1, 128), F32),
                jax.ShapeDtypeStruct((rows, features), BF16),
                jax.ShapeDtypeStruct((rows, features), BF16),
            ),
            in_specs=[anywhere] * 4,
            out_specs=(anywhere,) * 4,
            scratch_shapes=[dma((11,))],
            compiler_params=pltpu.CompilerParams(vmem_limit_bytes=8 * 1024 * 1024),
        )(corr, loss, ga, gb)
        return corr, loss[0, 0], ga, gb

    return jax.shard_map(
        on_device,
        mesh=mesh,
        in_specs=(P(("wide", "narrow"), None), P(("wide", "narrow"), None)),
        out_specs=(
            P("wide", "narrow"),
            P(),
            P(("wide", "narrow"), None),
            P(("wide", "narrow"), None),
        ),
        check_vma=False,
    )
```

```python
import functools

import jax
import jax.numpy as jnp
from jax import lax
from jax.experimental import pallas as pl
from jax.experimental.pallas import tpu as pltpu
from jax.sharding import PartitionSpec as P

off_weight = 0.0051
epsilon = 1e-05
MESH = pl.DeviceIdType.MESH
F32 = jnp.float32
BF16 = jnp.bfloat16


def kernel(
    WN, NN, BLK, SAMPLES,
    a_hbm, b_hbm,
    corr_ref, loss_ref, ga_ref, gb_ref,
    a_ref, b_ref, dummy,
    xa, xb, xb2, xa2,
    A3, B3, b1w, a1n,
    S_a, S_b, SR_a,
    gas, gar, gaall, gbs, gbr, gball,
    va, vb, Dn, Dw,
    dA, dB,
    mas, mar, mbs, mbr, ea, eb,
    ras, rar, rbs, rbr,
    lbuf, lsend, lrecv,
    s_w, r_w, s_n, r_n, r_a, r_b, r_d, in_sem,
):
    SLAB = BLK * (NN // WN)
    HB, HS = BLK // 2, SLAB // 2
    HN = SAMPLES // 2
    FEATS = BLK * NN
    w = lax.axis_index("wide")
    n = lax.axis_index("narrow")
    diag = lax.div(n, 2) == w

    z, y = lax.div(n, 4), lax.rem(n, 4)
    x, core = lax.div(w, 2), lax.rem(w, 2)

    def offset(j):
        return lax.rem(2 + 3 * j + 3 * lax.div(j * (j - 1), 2), 4)

    def wide_peer(i):
        return lax.rem(x + offset(lax.div(i, 2)), 4) * 2 + lax.rem(core + 1 - lax.rem(i, 2), 2)

    def narrow_peer(i):
        return lax.rem(z + offset(lax.div(i, 4)), 4) * 4 + lax.rem(y + offset(lax.rem(i, 4)), 4)

    def wide_copy(which, k, src, dst):
        return pltpu.make_async_remote_copy(
            src_ref=src, dst_ref=dst, send_sem=s_w.at[which], recv_sem=r_w.at[which],
            device_id=(wide_peer(k), n), device_id_type=MESH,
        )

    def narrow_copy(which, k, src, dst):
        return pltpu.make_async_remote_copy(
            src_ref=src, dst_ref=dst, send_sem=s_n.at[which], recv_sem=r_n.at[which],
            device_id=(w, narrow_peer(k)), device_id_type=MESH,
        )

    def each(count, body):
        def step(k, c):
            body(k)
            return c
        lax.fori_loop(0, count - 1, step, 0)


    def wide_recv(which, dst):
        ref = dst.at[pl.ds(0, WN - 1)]
        wide_copy(which, 1, ref, ref).wait_recv()

    def narrow_recv(which, dst):
        ref = dst.at[pl.ds(0, NN - 1)]
        narrow_copy(which, 1, ref, ref).wait_recv()

    def wide_sent(which, dst):
        ref = dst.at[pl.ds(0, WN - 1)]
        wide_copy(which, 1, ref, ref).wait_send()

    def narrow_sent(which, dst):
        ref = dst.at[pl.ds(0, NN - 1)]
        narrow_copy(which, 1, ref, ref).wait_send()

    def wide_a2a(which, src, dst):
        each(WN, lambda k: wide_copy(which, k, src.at[wide_peer(k)], dst.at[w]).start())

    def narrow_a2a(which, src, dst):
        each(NN, lambda k: narrow_copy(which, k, src.at[narrow_peer(k)], dst.at[n]).start())

    def wide_bcast(which, src, dst):
        each(WN, lambda k: wide_copy(which, k, src, dst.at[w]).start())

    def narrow_bcast(which, src, dst):
        each(NN, lambda k: narrow_copy(which, k, src, dst.at[n]).start())

    loads = [
        pltpu.make_async_copy(a_hbm, a_ref, in_sem.at[0]),
        pltpu.make_async_copy(b_hbm, b_ref, in_sem.at[1]),
    ]
    for load in loads:
        load.start()
    barrier = pltpu.get_barrier_semaphore()
    each(WN, lambda k: pl.semaphore_signal(
        barrier, inc=1, device_id=(wide_peer(k), n), device_id_type=MESH))
    each(NN, lambda k: pl.semaphore_signal(
        barrier, inc=1, device_id=(w, narrow_peer(k)), device_id_type=MESH))

    for load in loads:
        load.wait()

    def stack(ref, base, half):
        return jnp.concatenate(
            [ref[:, base:base + half], ref[:, base + half:base + 2 * half]], axis=0)

    for i in range(WN):
        xa[i] = stack(a_ref, i * SLAB, HS)
    for i in range(NN):
        xb[i] = stack(b_ref, i * BLK, HB)
    pl.semaphore_wait(barrier, WN + NN - 2)

    narrow_a2a(0, xb, B3.at[w])
    wide_a2a(0, xa, A3.at[n])
    A3[n, w] = xa[w]
    B3[w, n] = xb[n]
    for i in range(WN):
        xb2[i] = stack(b_ref, i * SLAB, HS)
    for i in range(NN):
        xa2[i] = stack(a_ref, i * BLK, HB)
    b1w[w] = xb2[w]
    a1n[n] = xa2[n]
    PART = WN // 2
    FULL, FIRST, SECOND = (0, PART), (0, PART // 2), (PART // 2, PART // 2)

    def slot(part, p, q):
        dz, dy = (q, p) if part == 0 else (p, q)
        return lax.rem(z + dz + 4, 4) * 4 + lax.rem(y + dy + 4, 4)

    def piece(part, at, cut):
        return A3.at[at, pl.ds(part * PART + cut[0], cut[1])]

    def move(part, index, at, cut, p, q):
        ref = piece(part, at, cut)
        return pltpu.make_async_remote_copy(
            src_ref=ref, dst_ref=ref, send_sem=s_n.at[1], recv_sem=r_a.at[part, index],
            device_id=(w, slot(part, p, q)), device_id_type=MESH,
        )

    LINES = (0, -1, 1, 2)

    def along(part, line, p, stage):
        step = (lambda d: (d, 0)) if stage == 1 else (lambda d: (0, d))
        for d, index in ((2, 3), (1, 0), (-1, 1)) if line == 3 else ((1, 0), (-1, 1)):
            move(part, line * 4 + index, slot(part, p, 0), FULL, *step(d)).start()

    def relay(part, line, p, stage):
        for d, index, cut in ((1, 2, FIRST), (-1, 3, SECOND)):
            got = slot(part, -d, 0) if stage == 1 else slot(part, p, -d)
            step = (d, 0) if stage == 1 else (0, d)
            move(part, line * 4 + index - 2, got, FULL, 0, 0).wait_recv()
            if line != 3:
                move(part, line * 4 + index, got, cut, *step).start()

    def far(part, line, p, stage):
        got = slot(part, 2, 0) if stage == 1 else slot(part, p, 2)
        for index, cut in ((3, FULL),) if line == 3 else ((2, FIRST), (3, SECOND)):
            move(part, line * 4 + index, got, cut, 0, 0).wait_recv()

    def move_b(index, at, dx, other):
        ref = B3.at[at]
        to = lax.rem(x + dx + 4, 4) * 2 + (1 - core if other else core)
        return pltpu.make_async_remote_copy(
            src_ref=ref, dst_ref=ref, send_sem=s_w.at[1], recv_sem=r_b.at[index],
            device_id=(to, n), device_id_type=MESH,
        )

    def slot_b(dx, other):
        return lax.rem(x + dx + 4, 4) * 2 + (1 - core if other else core)

    wide_recv(0, A3.at[n])
    for part in (0, 1):
        along(part, 4, 0, 1)
    for part in (0, 1):
        along(part, 0, 0, 2)
    narrow_recv(0, B3.at[w])
    for i, dx in ((2, 2), (0, 1), (1, -1)):
        move_b(i, w, dx, False).start()
    move_b(3, w, 0, True).start()
    def add_sums(ref, sums):
        def step(i, c):
            v = ref[i].astype(F32)
            return (c[0] + v, c[1] + v * v)
        return lax.fori_loop(0, ref.shape[0], step, sums, unroll=min(4, ref.shape[0]))

    def moments_of(sums):
        total, squares = sums

        def fold(t):
            return [jnp.sum(t[h * 8:(h + 1) * 8], axis=0, keepdims=True) / SAMPLES for h in (0, 1)]
        means, seconds = fold(total), fold(squares)
        invs = [lax.rsqrt(q - m * m + epsilon) for q, m in zip(seconds, means)]
        return means, invs

    def stacked(halves):
        return jnp.concatenate([jnp.broadcast_to(h, (8, h.shape[1])) for h in halves], axis=0)

    zero_b, zero_a = jnp.zeros((16, HB), F32), jnp.zeros((16, HS), F32)
    sums_b = add_sums(B3.at[w], (zero_b, zero_b))
    sums_a = add_sums(A3.at[n], (zero_a, zero_a))
    for part in (0, 1):
        relay(part, 4, 0, 1)
    for part in (0, 1):
        for line in (1, 2):
            along(part, line, LINES[line], 2)

    def take_b(i, dx, sums):
        got = slot_b(-dx, False)
        move_b(i, got, 0, False).wait_recv()
        move_b(4 + i, got, 0, True).start()
        return add_sums(B3.at[got], sums)

    def sums_of_piece(part, at, sums):
        return add_sums(piece(part, at, FULL), sums)

    for part in (0, 1):
        for p in (-1, 1):
            sums_a = sums_of_piece(part, slot(part, p, 0), sums_a)
    for part in (0, 1):
        relay(part, 0, 0, 2)
    for part in (0, 1):
        far(part, 4, 0, 1)
        along(part, 3, 2, 2)
    for i, dx in ((0, 1), (1, -1)):
        sums_b = take_b(i, dx, sums_b)
    for part in (0, 1):
        for line in (1, 2):
            relay(part, line, LINES[line], 2)
    sums_b = take_b(2, 2, sums_b)
    for i, dx in ((3, 0), (4, 1), (5, -1), (6, 2)):
        move_b(i, slot_b(-dx, True), 0, True).wait_recv()
        sums_b = add_sums(B3.at[slot_b(-dx, True)], sums_b)
    mean_b, inv_b = moments_of(sums_b)
    mean2, inv2 = stacked(mean_b), stacked(inv_b)

    def norm_b(i, c):
        src, pair = lax.div(i, NN // 2), lax.rem(i, NN // 2)
        even = (B3[src, 2 * pair].astype(F32) - mean2) * inv2
        odd = (B3[src, 2 * pair + 1].astype(F32) - mean2) * inv2
        at = pl.ds(pl.multiple_of(i * 16, 16), 16)
        for h in (0, 1):
            S_b[at, h * HB:(h + 1) * HB] = jnp.concatenate(
                [even[h * 8:h * 8 + 8], odd[h * 8:h * 8 + 8]], axis=0).astype(BF16)
        return c
    lax.fori_loop(0, SAMPLES // 16, norm_b, 0, unroll=2)

    dot_last = functools.partial(
        lax.dot_general, dimension_numbers=(((1,), (1,)), ((), ())), preferred_element_type=F32)

    def stack_gram(dst, g):
        count = g.shape[0] // 8
        g3 = g.reshape(count, 8, SAMPLES)
        dst[...] = jnp.concatenate([g3[:, :, :HN], g3[:, :, HN:]], axis=1).astype(BF16)

    own_rows = S_b[pl.ds(pl.multiple_of(w * NN * 8, 16), NN * 8), :]
    stack_gram(gbs, dot_last(own_rows, S_b[...]))
    narrow_a2a(3, gbs, gbr)
    gbr[n] = gbs[n]
    for part in (0, 1):
        relay(part, 3, 2, 2)
    wide_a2a(2, xb2, b1w)
    narrow_a2a(2, xa2, a1n)

    for part in (0, 1):
        for q in (-1, 1):
            sums_a = sums_of_piece(part, slot(part, 0, q), sums_a)
            for p in (-1, 1):
                sums_a = sums_of_piece(part, slot(part, p, q), sums_a)
        sums_a = sums_of_piece(part, slot(part, 2, 0), sums_a)
    for part in (0, 1):
        for q in (-1, 1):
            sums_a = sums_of_piece(part, slot(part, 2, q), sums_a)
    for line in range(4):
        for part in (0, 1):
            far(part, line, LINES[line], 2)
            sums_a = sums_of_piece(part, slot(part, LINES[line], 2), sums_a)
    mean_a, inv_a = moments_of(sums_a)
    mean2a, inv2a = stacked(mean_a), stacked(inv_a)

    def norm_a(i, c):
        src, pair = lax.div(i, NN // 2), lax.rem(i, NN // 2)
        even = (A3[2 * pair, src].astype(F32) - mean2a) * inv2a
        odd = (A3[2 * pair + 1, src].astype(F32) - mean2a) * inv2a
        at = pl.ds(pl.multiple_of(i * 16, 16), 16)
        for h in (0, 1):
            S_a[at, h * HS:(h + 1) * HS] = jnp.concatenate(
                [even[h * 8:h * 8 + 8], odd[h * 8:h * 8 + 8]], axis=0).astype(BF16)
        return c
    lax.fori_loop(0, SAMPLES // 16, norm_a, 0)
    for i in range(WN // 2):
        even = (A3[n, 2 * i].astype(F32) - mean2a) * inv2a
        odd = (A3[n, 2 * i + 1].astype(F32) - mean2a) * inv2a
        for h in (0, 1):
            SR_a[i * 16:i * 16 + 16, h * HS:(h + 1) * HS] = jnp.concatenate(
                [even[h * 8:h * 8 + 8], odd[h * 8:h * 8 + 8]], axis=0).astype(BF16)

    stack_gram(gas, dot_last(SR_a[...], S_a[...]))
    wide_a2a(3, gas, gar)
    gar[w] = gas[w]

    ones = jnp.ones((8, SAMPLES), BF16)
    mstd_a = jnp.dot(ones, S_a[...], preferred_element_type=F32) / SAMPLES
    mstd_b = jnp.dot(ones, S_b[...], preferred_element_type=F32) / SAMPLES

    half = lax.rem(n, 2)
    lbuf[...] = jnp.zeros_like(lbuf)
    ea[...] = jnp.zeros_like(ea)
    eb[...] = jnp.zeros_like(eb)

    def narrow_vec(k, h=None):
        h = half if h is None else h
        return pltpu.make_async_remote_copy(
            src_ref=vb, dst_ref=Dw.at[h], send_sem=s_n.at[4], recv_sem=r_d.at[h],
            device_id=(w, narrow_peer(k)), device_id_type=MESH,
        )

    @pl.when(diag)
    def _():
        def step(i, c):
            at = pl.ds(pl.multiple_of(i * 16, 16), 16)
            cols = pl.ds(pl.multiple_of(half * BLK, BLK), BLK)
            return c + S_a[at, cols].astype(F32) * S_b[at, :].astype(F32)
        prod = lax.fori_loop(0, SAMPLES // 16, step, jnp.zeros((16, BLK), F32), unroll=4)
        c = jnp.sum(prod, axis=0, keepdims=True) / SAMPLES
        d = -2.0 * (1.0 - c) - 2.0 * off_weight * c
        mb = jnp.concatenate(mean_b, axis=1)
        ib = jnp.concatenate(inv_b, axis=1)
        first = (half == 0).astype(F32)
        ma = mean_a[0] * first + mean_a[1] * (1.0 - first)
        ia = inv_a[0] * first + inv_a[1] * (1.0 - first)
        msa = mstd_a[0:1, :BLK] * first + mstd_a[0:1, BLK:] * (1.0 - first)
        pad = jnp.zeros((6, BLK), F32)
        ea[half] = jnp.concatenate([d * mstd_b[0:1], d * c, pad], axis=0)
        eb[...] = jnp.concatenate([d * msa, d * c, pad], axis=0)
        pad = jnp.zeros((5, BLK), F32)
        va[...] = jnp.concatenate([ma, ia, d, pad], axis=0)
        vb[...] = jnp.concatenate([mb, ib, d, pad], axis=0)
        Dn[...] = va[...]
        Dw[half] = vb[...]
        lbuf[0:1, :] = (1.0 - c) * (1.0 - c) - off_weight * c * c
        each(WN, lambda k: wide_copy(4, k, va, Dn).start())
        each(NN, lambda k: narrow_vec(k).start())

    def diag_recv():
        @pl.when(lax.div(n, 2) != w)
        def _():
            wide_copy(4, 1, va, Dn).wait_recv()
        for h in (0, 1):
            @pl.when(n != 2 * w + h)
            def _():
                narrow_vec(1, h).wait_recv()

    def diag_sent():
        @pl.when(diag)
        def _():
            ref = dummy.at[pl.ds(0, WN - 1)]
            wide_copy(4, 1, ref, ref).wait_send()
            ref = dummy.at[pl.ds(0, NN - 1)]
            narrow_copy(4, 1, ref, ref).wait_send()

    TM = SLAB // 2
    acc = jnp.zeros((8, BLK), F32)
    fb = jnp.zeros((8, BLK), F32)
    ones = jnp.ones((8, BLK), BF16)
    msb = mstd_b.astype(BF16)
    fa, sa = [], []
    for t in range(2):
        at = slice(t * TM, (t + 1) * TM)
        c = lax.dot_general(
            S_a[:, at], S_b[...], (((0,), (0,)), ((), ())), preferred_element_type=F32
        ) * (1.0 / SAMPLES)
        rounded = c.astype(BF16)
        corr_ref[at, :] = rounded
        squares = c * c
        acc = acc + jnp.sum(squares.reshape(TM // 8, 8, BLK), axis=0)
        fa.append(dot_last(msb, rounded)[0:1])
        sa.append(dot_last(ones, squares.astype(BF16))[0:1])
        fb = fb + jnp.dot(mstd_a[:, at].astype(BF16), rounded, preferred_element_type=F32)
    twice = 2.0 * off_weight
    m1 = jnp.concatenate([twice * fa[h] + ea[h, 0:1] for h in (0, 1)], axis=1)
    m2 = jnp.concatenate([twice * sa[h] + ea[h, 1:2] for h in (0, 1)], axis=1)
    Q = SLAB // 4
    lost = lbuf[...] + off_weight * acc
    mas[...] = jnp.concatenate(
        [jnp.concatenate([m[:, q * Q:(q + 1) * Q] for m in (m1, m2) for q in range(4)], axis=0)]
        + [sum(lost[:, q * 128:(q + 1) * 128] for q in range(BLK // 128))], axis=1)
    narrow_bcast(6, mas, mar)
    mar[n] = mas[...]
    m1 = twice * fb[0:1] + eb[0:1]
    m2 = twice * jnp.sum(acc, axis=0, keepdims=True) + eb[1:2]
    QB = BLK // 4
    mbs[...] = jnp.concatenate(
        [m[:, q * QB:(q + 1) * QB] for m in (m1, m2) for q in range(4)], axis=0)
    wide_bcast(6, mbs, mbr)
    mbr[w] = mbs[...]

    def total_of(ref):
        t = ref[0].astype(F32)
        for i in range(1, ref.shape[0]):
            t = t + ref[i].astype(F32)
        return t
    narrow_recv(3, gbr)
    gball[w] = total_of(gbr).astype(BF16)
    wide_bcast(5, gball.at[w], gball)
    wide_recv(3, gar)
    gaall[n] = total_of(gar).astype(BF16)
    narrow_bcast(5, gaall.at[n], gaall)

    wide_recv(2, b1w)
    narrow_recv(2, a1n)

    diag_recv()

    dmean, dinv, dd = (stacked([Dw[h, i:i + 1, :] for h in (0, 1)]) for i in range(3))
    for i in range(WN):
        s = ((b1w[i].astype(F32) - dmean) * dinv).astype(BF16).astype(F32) * dd
        for h in (0, 1):
            dA[i * 8:i * 8 + 8, h * HS:(h + 1) * HS] = s[h * 8:h * 8 + 8]
    dmean, dinv, dd = (
        stacked([Dn[i:i + 1, h * HB:(h + 1) * HB] for h in (0, 1)]) for i in range(3))
    for i in range(NN):
        s = ((a1n[i].astype(F32) - dmean) * dinv).astype(BF16).astype(F32) * dd
        for h in (0, 1):
            dB[i * 8:i * 8 + 8, h * HB:(h + 1) * HB] = s[h * 8:h * 8 + 8]

    factor = 2.0 * off_weight / SAMPLES

    def unstack(ref):
        g = ref[...].astype(F32)
        rows = ref.shape[0] * 8
        return [g[:, h * 8:h * 8 + 8, :].reshape(rows, HN).astype(BF16) for h in (0, 1)]

    def sum_messages(ref):
        t = ref[0]
        for i in range(1, ref.shape[0]):
            t = t + ref[i]
        return t

    wide_recv(5, gball)
    g0, g1 = unstack(gball)
    d = factor * (
        jnp.dot(g0, S_a[:HN, :], preferred_element_type=F32)
        + jnp.dot(g1, S_a[HN:, :], preferred_element_type=F32)
    ) + dA[...]
    narrow_recv(6, mar)
    total = sum_messages(mar)
    m1 = jnp.concatenate([total[q:q + 1, :Q] for q in range(4)], axis=1)
    m2 = jnp.concatenate([total[q + 4:q + 5, :Q] for q in range(4)], axis=1)
    inv = jnp.concatenate(inv_a, axis=1)
    grad = inv * (d - m1 - SR_a[...].astype(F32) * m2)
    for i in range(WN):
        ras[i] = jnp.concatenate(
            [grad[i * 8:i * 8 + 8, h * HS:(h + 1) * HS] for h in (0, 1)], axis=0).astype(BF16)
    wide_a2a(7, ras, rar)
    rar[w] = ras[w]
    lsend[...] = total[:, Q:]
    wide_bcast(8, lsend, lrecv)
    lrecv[w] = lsend[...]

    wide_recv(6, mbr)
    total = sum_messages(mbr)
    m1 = jnp.concatenate([total[q:q + 1] for q in range(4)], axis=1)
    m2 = jnp.concatenate([total[q + 4:q + 5] for q in range(4)], axis=1)
    inv = jnp.concatenate(inv_b, axis=1)
    own = pl.ds(pl.multiple_of(w * NN * 8, 16), NN * 8)
    rest = dB[...] - m1 - S_b[own, :].astype(F32) * m2
    narrow_recv(5, gaall)
    g0, g1 = unstack(gaall)
    d = factor * (
        jnp.dot(g0, S_b[:HN, :], preferred_element_type=F32)
        + jnp.dot(g1, S_b[HN:, :], preferred_element_type=F32)
    )
    grad = inv * (d + rest)
    for i in range(NN):
        rbs[i] = jnp.concatenate(
            [grad[i * 8:i * 8 + 8, h * HB:(h + 1) * HB] for h in (0, 1)], axis=0).astype(BF16)
    narrow_a2a(7, rbs, rbr)
    rbr[n] = rbs[n]

    wide_recv(7, rar)
    for i in range(WN):
        for h in (0, 1):
            ga_ref[:, i * SLAB + h * HS:i * SLAB + (h + 1) * HS] = rar[i, h * 8:h * 8 + 8, :]
    wide_recv(8, lrecv)
    loss = jnp.sum(sum_messages(lrecv), keepdims=True) / FEATS
    loss_ref[...] = jnp.broadcast_to(loss, loss_ref.shape)
    narrow_recv(7, rbr)
    for i in range(NN):
        for h in (0, 1):
            gb_ref[:, i * BLK + h * HB:i * BLK + (h + 1) * HB] = rbr[i, h * 8:h * 8 + 8, :]

    wide_sent(0, A3.at[n])
    narrow_sent(0, B3.at[w])
    wide_sent(1, B3)
    narrow_sent(1, A3)
    wide_sent(2, b1w)
    narrow_sent(2, a1n)
    wide_sent(3, gar)
    narrow_sent(3, gbr)
    diag_sent()
    wide_sent(5, gball)
    narrow_sent(5, gaall)
    wide_sent(6, mbr)
    narrow_sent(6, mar)
    wide_sent(7, rar)
    narrow_sent(7, rbr)
    wide_sent(8, lrecv)


def write_out(corr, loss, ga, gb, corr_out, loss_out, ga_out, gb_out, sem):
    rows = corr.shape[0] // 8
    copies = [
        pltpu.make_async_copy(
            corr.at[pl.ds(i * rows, rows)], corr_out.at[pl.ds(i * rows, rows)], sem.at[i])
        for i in range(8)
    ]
    copies.append(pltpu.make_async_copy(ga, ga_out, sem.at[8]))
    copies.append(pltpu.make_async_copy(gb, gb_out, sem.at[9]))
    copies.append(pltpu.make_async_copy(loss.at[pl.ds(0, 1)], loss_out, sem.at[10]))
    for copy in copies:
        copy.start()
    for copy in copies:
        copy.wait()


def solution(mesh):
    WN, NN = mesh.shape["wide"], mesh.shape["narrow"]

    def on_device(view_a, view_b):
        rows, features = view_a.shape
        samples = rows * WN * NN
        BLK = features // NN
        SLAB = features // WN
        HB, HS, HN = BLK // 2, SLAB // 2, samples // 2
        V = pltpu.VMEM
        vmem = pl.BlockSpec(memory_space=pltpu.VMEM)
        hbm = pl.BlockSpec(memory_space=pltpu.HBM)
        anywhere = pl.BlockSpec(memory_space=pl.ANY)
        dma = pltpu.SemaphoreType.DMA
        corr, loss, ga, gb = pl.pallas_call(
            functools.partial(kernel, WN, NN, BLK, samples),
            out_shape=(
                V((SLAB, BLK), BF16),
                V((8, 128), F32),
                V((rows, features), BF16),
                V((rows, features), BF16),
            ),
            in_specs=[hbm, hbm],
            out_specs=(vmem, vmem, vmem, vmem),
            scratch_shapes=[
                V((rows, features), BF16), V((rows, features), BF16), V((NN, 8, BLK), F32),
                V((WN, 16, HS), BF16), V((NN, 16, HB), BF16),
                V((WN, 16, HS), BF16), V((NN, 16, HB), BF16),
                V((NN, WN, 16, HS), BF16), V((WN, NN, 16, HB), BF16),
                V((WN, 16, HS), BF16), V((NN, 16, HB), BF16),
                V((samples, SLAB), BF16), V((samples, BLK), BF16), V((WN * 8, SLAB), BF16),
                V((WN, 16, HN), BF16), V((WN, 16, HN), BF16), V((NN, 16, HN), BF16),
                V((NN, 16, HN), BF16), V((NN, 16, HN), BF16), V((WN, 16, HN), BF16),
                V((8, BLK), F32), V((8, BLK), F32), V((8, BLK), F32), V((2, 8, BLK), F32),
                V((WN * 8, SLAB), F32), V((NN * 8, BLK), F32),
                V((8, SLAB // 4 + 128), F32), V((NN, 8, SLAB // 4 + 128), F32),
                V((8, BLK // 4), F32), V((WN, 8, BLK // 4), F32),
                V((2, 8, BLK), F32), V((8, BLK), F32),
                V((WN, 16, HS), BF16), V((WN, 16, HS), BF16),
                V((NN, 16, HB), BF16), V((NN, 16, HB), BF16),
                V((8, BLK), F32), V((8, 128), F32), V((WN, 8, 128), F32),
                dma((9,)), dma((9,)), dma((9,)), dma((9,)),
                dma((2, 20)), dma((7,)), dma((2,)), dma((2,)),
            ],
            compiler_params=pltpu.CompilerParams(
                collective_id=0, has_side_effects=True, vmem_limit_bytes=32 * 1024 * 1024),
        )(*(pltpu.with_memory_space_constraint(v, pltpu.HBM) for v in (view_a, view_b)))
        corr, loss, ga, gb = pl.pallas_call(
            write_out,
            out_shape=(
                jax.ShapeDtypeStruct((SLAB, BLK), BF16),
                jax.ShapeDtypeStruct((1, 128), F32),
                jax.ShapeDtypeStruct((rows, features), BF16),
                jax.ShapeDtypeStruct((rows, features), BF16),
            ),
            in_specs=[anywhere] * 4,
            out_specs=(anywhere,) * 4,
            scratch_shapes=[dma((11,))],
            compiler_params=pltpu.CompilerParams(vmem_limit_bytes=8 * 1024 * 1024),
        )(corr, loss, ga, gb)
        return corr, loss[0, 0], ga, gb

    return jax.shard_map(
        on_device,
        mesh=mesh,
        in_specs=(P(("wide", "narrow"), None), P(("wide", "narrow"), None)),
        out_specs=(
            P("wide", "narrow"),
            P(),
            P(("wide", "narrow"), None),
            P(("wide", "narrow"), None),
        ),
        check_vma=False,
    )
```
